32 devices in a mesh: groups: 2 (over y), shot: 4 (over z), sub: 2 (over x), rep: 2 (over core).
Axes of the slice: x: 2, y: 2, z: 4, core: 2. Of those that a mesh axis runs over, the one named last changes fastest.
Arguments:
- model: float32 [256, 3, 640], P(('groups', 'shot')), parts along dimension 0, may hold values from 1 to 2.5
- accum: float32 [256, 3, 640], P(('groups', 'shot')), parts along dimension 0, may hold values from 1 to 100
- owner_map: int32 [256], P('groups'), parts along dimension 0, may hold values from 0 to 127, as said below
- aperture: int32 [8, 2, 32], P('groups', 'sub'), parts along dimension 0, may hold values from 0 to 127, as said below
- start_state: bfloat16 [8, 2, 1, 9, 16, 80, 32], P(('groups', 'shot'), 'rep', None, None, 'sub'), parts along dimension 0, may hold values from -6 to 6
- adjoint_end: bfloat16 [8, 2, 1, 9, 16, 80, 32], P(('groups', 'shot'), 'rep', None, None, 'sub'), parts along dimension 0, may hold values from -6 to 6
- wavelet: float32 [8, 2, 1, 2], P(('groups', 'shot'), 'rep'), parts along dimension 0, may hold values from -24 to 24
- source_cell: int32 [8, 2, 1], P(('groups', 'shot'), 'rep'), parts along dimension 0, may hold values from 0 to 40959
- receiver_cell: int32 [8, 2, 1, 256], P(('groups', 'shot'), 'rep'), parts along dimension 0, may hold values from 0 to 40959
- observed: float32 [8, 2, 1, 2, 256], P(('groups', 'shot'), 'rep'), parts along dimension 0, may hold values from -6 to 6
Outputs:
- new_model: float32 [256, 3, 640], P(('groups', 'shot')), parts along dimension 0
- new_accum: float32 [256, 3, 640], P(('groups', 'shot')), parts along dimension 0
The draws below stay inside these ranges and needn't reach their ends.
There are 2 independent parts, one for each index of `groups`. The reference program is written for one: setup_inputs(seed, part) draws one part's arguments, and reference() takes and returns one part's arrays. A program takes and returns all parts, laid end to end along the dimension named above; each array names one. Nothing has to cross between parts.
Inputs may be any that keep to these rules, and one draw needn't show every extreme that they name: `owner_map`: A permutation: each tile's storage slot; the owner of a tile is its slot // 32. The 32 ids of one slab aperture[s, u, :] are distinct; at most 16 of them have one owner, and in every slab some owner has exactly 16. All replicas of shot s share its aperture.
All inputs are finite; a program needn't handle non-finite values.
Results may differ from the reference program's by a relative error of at most 0.0003.
Values sent between devices are 32-bit elements; how exact they have to be, the bound alone decides.
A program may use at most 64 MiB of HBM per device.

```python
import math
import jax
import jax.numpy as jnp
from jax import lax

DEPTH = 32
TILE_X = 4
TILE_Y = 5
SLAB_XT = 2
SLAB_YT = 16
TILES_DEV = 32
SHOTS = 1
NSTEPS = 2
NREC = 256
SLAB_TILES = 32
TILE_CELLS = 640
WIDTH_Y = 80
APER_X = 16
NTILES = 128
PER_OWNER = 16
N_SHOT = 4
N_SUB = 2
N_REP = 2


def routing_tables(key):
    owner_map = jax.random.permutation(jax.random.fold_in(key, 101), NTILES).astype(jnp.int32)
    tile_of_slot = jnp.argsort(owner_map).astype(jnp.int32)
    slab_keys = jax.random.split(jax.random.fold_in(key, 202), N_SHOT * N_SUB)
    positions = jnp.arange(SLAB_TILES, dtype=jnp.int32)

    def one_slab(slab_key):
        first_key, second_key, third_key, fourth_key = jax.random.split(slab_key, 4)
        order = jax.random.permutation(first_key, N_SHOT).astype(jnp.int32)
        copies = jax.random.permutation(second_key, (N_SHOT - 1) * PER_OWNER)[:SLAB_TILES - PER_OWNER]
        busiest = jnp.zeros((PER_OWNER,), jnp.int32) + order[0]
        owners = jnp.concatenate([busiest, order[1 + copies // PER_OWNER]]).astype(jnp.int32)
        owners = jax.random.permutation(third_key, owners)
        earlier = (owners[None, :] == owners[:, None]) & (positions[None, :] < positions[:, None])
        ranks = jnp.sum(earlier.astype(jnp.int32), axis=1)
        offsets = jax.random.randint(fourth_key, (N_SHOT,), 0, TILES_DEV).astype(jnp.int32)
        local_rows = (offsets[owners] + ranks) % TILES_DEV
        return tile_of_slot[owners * TILES_DEV + local_rows]
    aperture = jax.vmap(one_slab)(slab_keys).reshape(N_SHOT, N_SUB, SLAB_TILES).astype(jnp.int32)
    return (owner_map, aperture)


def draw_owner_map(key, part):
    tables = routing_tables(key)
    return tables[0]


def draw_aperture(key, part):
    tables = routing_tables(key)
    return tables[1]


def place_ends(values, key, smallest, top_value):
    dims = values.shape
    spot = [jax.random.randint(jax.random.fold_in(key, axis), (), 0, dims[axis]) for axis in range(len(dims))]
    values = values.at[tuple(spot)].set(smallest)
    longest = dims.index(max(dims))
    spot[longest] = (spot[longest] + 1) % dims[longest]
    return values.at[tuple(spot)].set(top_value)


def level_of(rng, shape, shards, low, largest):
    def one(axis_at, parts):
        draws = jax.random.uniform(jax.random.fold_in(jax.random.fold_in(rng, 6), axis_at), (parts,), jnp.float32, low / len(shards), largest / len(shards))
        return jnp.repeat(jnp.exp(draws), shape[axis_at] // parts).reshape((-1,) + (1,) * (len(shape) - axis_at - 1))

    factor_of = one(*shards[0])
    for cut in shards[1:]:
        factor_of = factor_of * one(*cut)
    return factor_of


def scatter_about(rng, extent, spread, limit, pieces=(), held_as=jnp.bfloat16):
    result = jax.random.normal(rng, extent, jnp.float32) * spread
    if len(pieces) > 0:
        result = level_of(rng, extent, pieces, -0.22, 0.18) * result
    return jnp.clip(result, min=-limit, max=limit).astype(held_as)


def setup_inputs(seed: int = 0, part: int = 0) -> dict:
    key_list = jax.random.split(jax.random.key(seed), 11)
    own_keys = jax.random.split(jax.random.fold_in(key_list[10], part), 11)
    model = jnp.clip(1.0 + 1.5 * jax.random.uniform(own_keys[0], (NTILES, 3, TILE_CELLS), jnp.float32) ** level_of(own_keys[0], (NTILES, 3, TILE_CELLS), ((0, 4),), -0.2, 0.2), 1.0, 2.5)
    accum = jnp.clip(jnp.exp(math.log(100.0) - 4.6051702 * jax.random.uniform(own_keys[1], (NTILES, 3, TILE_CELLS), jnp.float32) ** level_of(own_keys[1], (NTILES, 3, TILE_CELLS), ((0, 4),), -0.2, 0.2)), 1.0, 100.0)
    owner_map = draw_owner_map(jax.random.fold_in(jax.random.fold_in(key_list[10], part), 71), part)
    aperture = draw_aperture(jax.random.fold_in(jax.random.fold_in(key_list[10], part), 71), part)
    start_state = scatter_about(own_keys[4], (N_SHOT, N_REP, SHOTS, 9, APER_X, WIDTH_Y, DEPTH), 1.0, 6.0, ((0, 4), (1, 2), (4, 2)))
    adjoint_end = scatter_about(own_keys[5], (N_SHOT, N_REP, SHOTS, 9, APER_X, WIDTH_Y, DEPTH), 1.0, 6.0, ((0, 4), (1, 2), (4, 2)))
    wavelet = scatter_about(own_keys[6], (N_SHOT, N_REP, SHOTS, NSTEPS), 4.0, 24.0, ((0, 4), (1, 2)), jnp.float32)
    source_cell = place_ends(jax.random.randint(own_keys[7], (N_SHOT, N_REP, SHOTS), 0, APER_X * WIDTH_Y * DEPTH), jax.random.fold_in(own_keys[7], 1), 0, (APER_X * WIDTH_Y * DEPTH) - 1).astype(jnp.int32)
    receiver_cell = place_ends(jax.random.randint(own_keys[8], (N_SHOT, N_REP, SHOTS, NREC), 0, APER_X * WIDTH_Y * DEPTH), jax.random.fold_in(own_keys[8], 1), 0, (APER_X * WIDTH_Y * DEPTH) - 1).astype(jnp.int32)
    observed = scatter_about(own_keys[9], (N_SHOT, N_REP, SHOTS, NSTEPS, NREC), 1.0, 6.0, ((0, 4), (1, 2)), jnp.float32)
    return dict(model=model, accum=accum, owner_map=owner_map, aperture=aperture, start_state=start_state, adjoint_end=adjoint_end, wavelet=wavelet, source_cell=source_cell, receiver_cell=receiver_cell, observed=observed)


time_step = 0.18
learn_rate = 0.5

def plus_x(field, right):
    return jnp.concatenate([field[:, 1:], right], axis=1) - field

def minus_x(field, left):
    return field - jnp.concatenate([left, field[:, :-1]], axis=1)

def plus_y(field):
    return jnp.concatenate([field[:, :, 1:], jnp.zeros_like(field[:, :, :1])], axis=2) - field

def minus_y(field):
    return field - jnp.concatenate([jnp.zeros_like(field[:, :, :1]), field[:, :, :-1]], axis=2)

def plus_z(field):
    return jnp.concatenate([field[:, :, :, 1:], jnp.zeros_like(field[:, :, :, :1])], axis=3) - field

def minus_z(field):
    return field - jnp.concatenate([jnp.zeros_like(field[:, :, :, :1]), field[:, :, :, :-1]], axis=3)

def velocity_half(state, density, left_rim, right_rim):
    buoyancy = 1.0 / density
    vel_x, vel_y, vel_z = (state[:, 0], state[:, 1], state[:, 2])
    stress_xx, stress_yy, stress_zz = (state[:, 3], state[:, 4], state[:, 5])
    stress_xy, stress_xz, stress_yz = (state[:, 6], state[:, 7], state[:, 8])
    new_x = vel_x + time_step * buoyancy * (plus_x(stress_xx, right_rim[:, 0]) + minus_y(stress_xy) + minus_z(stress_xz))
    new_y = vel_y + time_step * buoyancy * (minus_x(stress_xy, left_rim[:, 0]) + plus_y(stress_yy) + minus_z(stress_yz))
    new_z = vel_z + time_step * buoyancy * (minus_x(stress_xz, left_rim[:, 1]) + minus_y(stress_yz) + plus_z(stress_zz))
    return jnp.concatenate([jnp.stack([new_x, new_y, new_z], axis=1), state[:, 3:]], axis=1)

def stress_half(state, lame, shear, left_rim, right_rim):
    vel_x, vel_y, vel_z = (state[:, 0], state[:, 1], state[:, 2])
    strain_xx = minus_x(vel_x, left_rim[:, 0])
    strain_yy = minus_y(vel_y)
    strain_zz = minus_z(vel_z)
    volume = strain_xx + strain_yy + strain_zz
    new_xx = state[:, 3] + time_step * (lame * volume + 2.0 * shear * strain_xx)
    new_yy = state[:, 4] + time_step * (lame * volume + 2.0 * shear * strain_yy)
    new_zz = state[:, 5] + time_step * (lame * volume + 2.0 * shear * strain_zz)
    new_xy = state[:, 6] + time_step * shear * (plus_y(vel_x) + plus_x(vel_y, right_rim[:, 0]))
    new_xz = state[:, 7] + time_step * shear * (plus_z(vel_x) + plus_x(vel_z, right_rim[:, 1]))
    new_yz = state[:, 8] + time_step * shear * (plus_z(vel_y) + plus_y(vel_z))
    stresses = jnp.stack([new_xx, new_yy, new_zz, new_xy, new_xz, new_yz], axis=1)
    return jnp.concatenate([state[:, :3], stresses], axis=1)

def inject(state, onehot, amplitude):
    source = time_step * amplitude[:, None, None, None] * onehot
    return state.at[:, 3:6].add(source[:, None])

def shot_gradient(params, start, adjoint, amplitudes, onehot, receivers, observed):
    shots = start.shape[0]
    rim_one = jnp.zeros(start[:, :1, :1].shape, jnp.float32)
    rim_two = jnp.zeros(start[:, :2, :1].shape, jnp.float32)

    def objective(values):
        state = start
        misfit = jnp.zeros((), jnp.float32)
        for number in range(NSTEPS):
            state = velocity_half(state, values[2], rim_two, rim_one)
            state = stress_half(state, values[0], values[1], rim_one, rim_two)
            state = inject(state, onehot, amplitudes[:, number])
            recorded = jnp.take_along_axis(state[:, 2].reshape(shots, -1), receivers, axis=1)
            difference = recorded - observed[:, number]
            misfit = misfit + 0.5 * jnp.sum(difference * difference)
        return jnp.sum(adjoint * state) + misfit
    return jax.grad(objective)(params)

def reference(model, accum, owner_map, aperture, start_state, adjoint_end, wavelet, source_cell, receiver_cell, observed):
    slots = owner_map[aperture]
    cells = APER_X * WIDTH_Y * DEPTH
    shots = start_state.shape[2]

    def visit(total, device):
        shot = device // N_REP
        replica = device % N_REP
        slab_slots = slots[shot].reshape(-1)
        tiles = model[slab_slots]
        params = tiles.reshape(N_SUB, SLAB_XT, SLAB_YT, 3, TILE_X, TILE_Y, DEPTH)
        params = params.transpose(3, 0, 1, 4, 2, 5, 6).reshape(3, APER_X, WIDTH_Y, DEPTH)
        start = start_state[shot, replica].astype(jnp.float32)
        adjoint = adjoint_end[shot, replica].astype(jnp.float32)
        onehot = (jnp.arange(cells, dtype=jnp.int32)[None, :] == source_cell[shot, replica][:, None]).astype(jnp.float32)
        onehot = onehot.reshape(shots, APER_X, WIDTH_Y, DEPTH)
        gradient = shot_gradient(params, start, adjoint, wavelet[shot, replica], onehot, receiver_cell[shot, replica], observed[shot, replica])
        back = gradient.reshape(3, N_SUB, SLAB_XT, TILE_X, SLAB_YT, TILE_Y, DEPTH)
        back = back.transpose(1, 2, 4, 0, 3, 5, 6).reshape(N_SUB * SLAB_TILES, 3, TILE_CELLS)
        return (total.at[slab_slots].add(back), None)
    total, _ = lax.scan(visit, jnp.zeros(model.shape, jnp.float32), jnp.arange(N_SHOT * N_REP, dtype=jnp.int32))
    new_accum = accum + total * total
    new_model = model - learn_rate * total / jnp.sqrt(new_accum)
    return (new_model, new_accum)
```

```python
import functools
import jax
import jax.numpy as jnp
from jax import lax
from jax.experimental import pallas as pl
from jax.experimental.pallas import tpu as pltpu
from jax.sharding import PartitionSpec as P

DEPTH = 32
TILE_X = 4
TILE_Y = 5
SLAB_XT = 2
SLAB_YT = 16
NSTEPS = 2
SLAB_TILES = 32
LX = SLAB_XT * TILE_X
WY = SLAB_YT * TILE_Y
LANES = 128

time_step = 0.18
learn_rate = 0.5
MESH = pl.DeviceIdType.MESH
F32 = jnp.float32

TO_PRIOR = (2, 2, 1, 4, 1)
TO_NEXT = (4, 1, 2, 2, 2)


def next_y(f):
    return pltpu.roll(f, LANES - 1, 1)


def prior_y(f):
    return pltpu.roll(f, 1, 1)


def physics(
    start_ref, adj_ref, par_ref, wave_ref, src_ref, rec_ref, obs_ref, grad_ref,
    F, C, W, A, B, DV, ST, CNT, OB, R0,
    send_l, send_r, recv_l, recv_r, ss_l, ss_r, rs_l, rs_r,
):
    n_sub = lax.axis_size("sub")
    me = lax.axis_index("sub")
    has_l = me > 0
    has_r = me < n_sub - 1
    left = {"sub": jnp.maximum(me - 1, 0)}
    right = {"sub": jnp.minimum(me + 1, n_sub - 1)}
    barrier = pltpu.get_barrier_semaphore()

    @pl.when(has_l)
    def _():
        pl.semaphore_signal(barrier, inc=1, device_id=left, device_id_type=MESH)

    @pl.when(has_r)
    def _():
        pl.semaphore_signal(barrier, inc=1, device_id=right, device_id_type=MESH)

    @pl.when(has_l)
    def _():
        pl.semaphore_wait(barrier, 1)

    @pl.when(has_r)
    def _():
        pl.semaphore_wait(barrier, 1)

    def copies(e):
        nl, nr = TO_PRIOR[e], TO_NEXT[e]
        to_l = pltpu.make_async_remote_copy(
            src_ref=send_l.at[e, pl.ds(0, nl)], dst_ref=recv_r.at[e, pl.ds(0, nl)],
            send_sem=ss_l.at[e], recv_sem=rs_r.at[e], device_id=left, device_id_type=MESH)
        to_r = pltpu.make_async_remote_copy(
            src_ref=send_r.at[e, pl.ds(0, nr)], dst_ref=recv_l.at[e, pl.ds(0, nr)],
            send_sem=ss_r.at[e], recv_sem=rs_l.at[e], device_id=right, device_id_type=MESH)
        return to_l, to_r

    def send(e, firsts, lasts):
        to_l, to_r = copies(e)

        @pl.when(has_l)
        def _():
            for k, (ref, i) in enumerate(firsts):
                send_l[e, k] = ref[i, 1]
            to_l.start()

        @pl.when(has_r)
        def _():
            for k, (ref, i) in enumerate(lasts):
                send_r[e, k] = ref[i, LX]
            to_r.start()

    def receive(e, firsts, lasts):
        to_l, to_r = copies(e)

        @pl.when(has_r)
        def _():
            to_r.wait_send()
            to_l.wait_recv()
            for k, (ref, i) in enumerate(firsts):
                ref[i, LX + 1] = recv_r[e, k]

        @pl.when(has_l)
        def _():
            to_l.wait_send()
            to_r.wait_recv()
            for k, (ref, i) in enumerate(lasts):
                ref[i, 0] = recv_l[e, k]

    zrow = lax.broadcasted_iota(jnp.int32, (DEPTH, LANES), 0)
    lane = lax.broadcasted_iota(jnp.int32, (DEPTH, LANES), 1)
    inside = lane < WY

    def next_z(f):
        return jnp.where(zrow == DEPTH - 1, 0.0, pltpu.roll(f, DEPTH - 1, 0))

    def prior_z(f):
        return jnp.where(zrow == 0, 0.0, pltpu.roll(f, 1, 0))

    def py(f):
        return next_y(f) - f

    def my(f):
        return f - prior_y(f)

    def pz(f):
        return next_z(f) - f

    def mz(f):
        return f - prior_z(f)

    def px(ref, i, x):
        return ref[i, x + 1] - ref[i, x]

    def mx(ref, i, x):
        return ref[i, x] - ref[i, x - 1]

    zero = jnp.zeros((DEPTH, LANES), F32)

    def strain_cot(x, c):
        lame = par_ref[0, x - 1]
        shear = par_ref[1, x - 1]
        trace = time_step * lame * (c[0] + c[1] + c[2])
        ds = time_step * shear
        W[0, x] = trace + 2.0 * ds * c[0]
        W[1, x] = trace + 2.0 * ds * c[1]
        W[2, x] = trace + 2.0 * ds * c[2]
        W[3, x] = ds * c[3]
        W[4, x] = ds * c[4]
        W[5, x] = ds * c[5]

    def edges_first(body, after):
        body(1)
        body(LX)
        after()
        lax.fori_loop(2, LX, lambda x, _: (body(x), 0)[1], 0)

    for i in range(9):
        F[i, 0] = zero
        F[i, LX + 1] = zero
    for i in range(6):
        W[i, 0] = zero
        W[i, LX + 1] = zero
    for i in range(3):
        A[i, 0] = zero
        A[i, LX + 1] = zero

    def load(x):
        for i in range(9):
            F[i, x] = zero
            F[i, x, :, pl.ds(0, WY)] = start_ref[i, x - 1].astype(F32)
            C[i, x - 1] = zero
            C[i, x - 1, :, pl.ds(0, WY)] = adj_ref[i, x - 1].astype(F32)
        B[x - 1] = jnp.where(inside, 1.0 / jnp.where(inside, par_ref[2, x - 1], 1.0), 0.0)
        strain_cot(x, [C[3 + i, x - 1] for i in range(6)])

    e0 = ([(F, 3), (W, 0)], [(F, 6), (F, 7), (W, 3), (W, 4)])
    e1 = ([(F, 1), (F, 2)], [(F, 0)])
    e2 = ([(F, 3)], [(F, 6), (F, 7)])
    e3 = ([(F, 1), (F, 2), (A, 1), (A, 2)], [(F, 0), (A, 0)])
    e4 = ([(W, 0)], [(W, 3), (W, 4)])

    edges_first(load, lambda: send(0, *e0))

    cell = rec_ref[...]
    q = cell >> 5
    rx = (q * 52429) >> 22
    ry = q - rx * WY
    rrow = (rx - me * LX) * DEPTH + (cell & (DEPTH - 1))
    nrec = rec_ref.shape[1]
    rows = lax.broadcasted_iota(jnp.int32, (LX * DEPTH, nrec), 0)
    cols = lax.broadcasted_iota(jnp.int32, (LANES, nrec), 0)
    at_row = jnp.where(rows == rrow, 1.0, 0.0).astype(F32)
    at_col = cols == ry
    dims = (((1,), (1,)), ((), ()))

    def spread(values):
        return lax.dot_general(
            at_row, jnp.where(at_col, values, 0.0), dims,
            precision=lax.Precision.HIGHEST, preferred_element_type=F32)

    CNT[...] = spread(jnp.ones((1, nrec), F32)).reshape(LX, DEPTH, LANES)
    OB[0] = spread(obs_ref[0:1]).reshape(LX, DEPTH, LANES)
    OB[1] = spread(obs_ref[1:2]).reshape(LX, DEPTH, LANES)

    scell = src_ref[0]
    sq = scell >> 5
    sx = (sq * 52429) >> 22
    sy = sq - sx * WY
    sz = scell & (DEPTH - 1)
    at_src = jnp.where((zrow == sz) & (lane == sy), 1.0, 0.0)

    def divergence(x):
        return [
            px(F, 3, x) + my(F[6, x]) + mz(F[7, x]),
            mx(F, 6, x) + py(F[4, x]) + mz(F[8, x]),
            mx(F, 7, x) + my(F[8, x]) + pz(F[5, x]),
        ]

    def strains(x):
        vx, vy, vz = F[0, x], F[1, x], F[2, x]
        return [
            mx(F, 0, x), my(vy), mz(vz),
            py(vx) + px(F, 1, x), pz(vx) + px(F, 2, x), pz(vy) + py(vz),
        ]

    def velocity_cot(x):
        exx, eyy, ezz = W[0, x], W[1, x], W[2, x]
        gxy, gxz, gyz = W[3, x], W[4, x], W[5, x]
        return [
            px(W, 0, x) + my(gxy) + mz(gxz),
            py(eyy) + mx(W, 3, x) + mz(gyz),
            pz(ezz) + mx(W, 4, x) + my(gyz),
        ]

    def first_velocity(x):
        b = time_step * B[x - 1]
        d = divergence(x)
        for i in range(3):
            DV[i, x - 1] = d[i]
            F[i, x] = F[i, x] + b * d[i]
        R0[x - 1] = CNT[x - 1] * F[2, x] - OB[0, x - 1]

    receive(0, *e0)
    edges_first(first_velocity, lambda: send(1, *e1))

    def first_stress(x):
        lame = time_step * par_ref[0, x - 1]
        shear = time_step * par_ref[1, x - 1]
        s = strains(x)
        for i in range(6):
            ST[i, x - 1] = s[i]
        amp = jnp.where(x - 1 + me * LX == sx, time_step * wave_ref[0], 0.0)
        base = lame * (s[0] + s[1] + s[2]) + amp * at_src
        for i in range(3):
            F[3 + i, x] = F[3 + i, x] + (base + 2.0 * shear * s[i])
            F[6 + i, x] = F[6 + i, x] + shear * s[3 + i]

    receive(1, *e1)
    edges_first(first_stress, lambda: send(2, *e2))

    def second_velocity(x):
        inv = B[x - 1]
        b = time_step * inv
        d = divergence(x)
        w = velocity_cot(x)
        for i in range(3):
            F[i, x] = F[i, x] + b * d[i]
        res = CNT[x - 1] * F[2, x] - OB[1, x - 1]
        total = zero
        for i in range(3):
            c = C[i, x - 1] - w[i]
            if i == 2:
                c = c + res
            C[i, x - 1] = c
            a = b * c
            A[i, x] = a
            total = total + a * d[i]
        grad_ref[2, x - 1] = -inv * total

    receive(2, *e2)
    edges_first(second_velocity, lambda: send(3, *e3))

    def model_part(c, s):
        part_lame = (s[0] + s[1] + s[2]) * (c[0] + c[1] + c[2])
        part_shear = 2.0 * (s[0] * c[0] + s[1] * c[1] + s[2] * c[2]) + (
            s[3] * c[3] + s[4] * c[4] + s[5] * c[5])
        return part_lame, part_shear

    def stress_back(x):
        c = [C[3 + i, x - 1] for i in range(6)]
        lame1, shear1 = model_part(c, strains(x))
        ax, ay, az = A[0, x], A[1, x], A[2, x]
        c = [
            c[0] - mx(A, 0, x),
            c[1] - my(ay),
            c[2] - mz(az),
            c[3] - py(ax) - px(A, 1, x),
            c[4] - pz(ax) - px(A, 2, x),
            c[5] - pz(ay) - py(az),
        ]
        strain_cot(x, c)
        lame0, shear0 = model_part(c, [ST[i, x - 1] for i in range(6)])
        grad_ref[0, x - 1] = time_step * (lame1 + lame0)
        grad_ref[1, x - 1] = time_step * (shear1 + shear0)

    receive(3, *e3)
    edges_first(stress_back, lambda: send(4, *e4))

    def last_velocity(x):
        inv = B[x - 1]
        b = time_step * inv
        w = velocity_cot(x)
        total = zero
        for i in range(3):
            c = C[i, x - 1] - w[i]
            if i == 2:
                c = c + R0[x - 1]
            total = total + b * c * DV[i, x - 1]
        grad_ref[2, x - 1] = grad_ref[2, x - 1] - inv * total

    receive(4, *e4)
    lax.fori_loop(1, LX + 1, lambda x, _: (last_velocity(x), 0)[1], 0)


def run_physics(start, adj, params, wave, src, rec, obs):
    vm = pl.BlockSpec(memory_space=pltpu.VMEM)
    sm = pl.BlockSpec(memory_space=pltpu.SMEM)
    layer = (DEPTH, LANES)
    halo = pltpu.VMEM((5, 4) + layer, F32)
    dma = pltpu.SemaphoreType.DMA((5,))
    return pl.pallas_call(
        physics,
        out_shape=jax.ShapeDtypeStruct((3, LX) + layer, F32),
        in_specs=[vm, vm, vm, sm, sm, vm, vm],
        out_specs=vm,
        scratch_shapes=[
            pltpu.VMEM((9, LX + 2) + layer, F32),
            pltpu.VMEM((9, LX) + layer, F32),
            pltpu.VMEM((6, LX + 2) + layer, F32),
            pltpu.VMEM((3, LX + 2) + layer, F32),
            pltpu.VMEM((LX,) + layer, F32),
            pltpu.VMEM((3, LX) + layer, F32),
            pltpu.VMEM((6, LX) + layer, F32),
            pltpu.VMEM((LX,) + layer, F32),
            pltpu.VMEM((2, LX) + layer, F32),
            pltpu.VMEM((LX,) + layer, F32),
            halo, halo, halo, halo, dma, dma, dma, dma,
        ],
        compiler_params=pltpu.CompilerParams(
            collective_id=0, has_side_effects=True, vmem_limit_bytes=40 * 1024 * 1024),
    )(start, adj, params, wave, src, rec, obs)


def on_device(
    model,
    accum,
    owner_map,
    aperture,
    start_state,
    adjoint_end,
    wavelet,
    source_cell,
    receiver_cell,
    observed,
):
    n_shot = lax.axis_size("shot")
    my_shot = lax.axis_index("shot")
    tiles_dev = model.shape[0]
    tile_cells = model.shape[2]
    per_owner = 2 * SLAB_TILES // n_shot
    slab_slots = owner_map[aperture[:, 0, :]]
    owners = slab_slots // tiles_dev
    local_rows = slab_slots % tiles_dev
    positions = jnp.arange(SLAB_TILES, dtype=jnp.int32)
    earlier = (owners[:, :, None] == owners[:, None, :]) & (
        positions[None, None, :] < positions[None, :, None]
    )
    ranks = jnp.sum(earlier.astype(jnp.int32), axis=2)
    slot_ids = jnp.arange(per_owner, dtype=jnp.int32)
    serve = (owners[:, None, :] == my_shot) & (ranks[:, None, :] == slot_ids[None, :, None])
    served = jnp.any(serve, axis=2)
    serve_rows = jnp.sum(jnp.where(serve, local_rows[:, None, :], 0), axis=2)
    outgoing = jnp.where(served[:, :, None, None], model[serve_rows], 0.0)
    incoming = lax.all_to_all(outgoing, "shot", split_axis=0, concat_axis=0, tiled=True)
    my_owners = owners[my_shot]
    my_ranks = ranks[my_shot]
    slab = incoming.reshape(n_shot * per_owner, 3, tile_cells)[my_owners * per_owner + my_ranks]
    slab_x = SLAB_XT * TILE_X
    slab_y = SLAB_YT * TILE_Y
    params = slab.reshape(SLAB_XT, SLAB_YT, 3, TILE_X, TILE_Y, DEPTH)
    params = params.transpose(2, 0, 3, 5, 1, 4).reshape(3, slab_x, DEPTH, slab_y)
    params = jnp.pad(params, ((0, 0), (0, 0), (0, 0), (0, LANES - slab_y)))
    start = start_state[0, 0, 0].transpose(0, 1, 3, 2)
    adj = adjoint_end[0, 0, 0].transpose(0, 1, 3, 2)
    gradient = run_physics(
        start, adj, params, wavelet.reshape(NSTEPS), source_cell.reshape(1),
        receiver_cell.reshape(1, -1), observed[0, 0, 0],
    )[..., :slab_y]
    back = gradient.reshape(3, SLAB_XT, TILE_X, DEPTH, SLAB_YT, TILE_Y)
    back = back.transpose(1, 4, 0, 2, 5, 3).reshape(SLAB_TILES, 3, tile_cells)
    all_slots = jnp.arange(per_owner, dtype=jnp.int32)
    owner_ids = jnp.arange(n_shot, dtype=jnp.int32)
    place = (my_owners[None, None, :] == owner_ids[:, None, None]) & (
        my_ranks[None, None, :] == all_slots[None, :, None]
    )
    placed = jnp.any(place, axis=2)
    place_rows = jnp.sum(jnp.where(place, positions[None, None, :], 0), axis=2)
    returning = jnp.where(placed[:, :, None, None], back[place_rows], 0.0)
    arrived = lax.all_to_all(returning, "shot", split_axis=0, concat_axis=0, tiled=True)
    pick = (
        serve_rows[:, :, None] == jnp.arange(tiles_dev, dtype=jnp.int32)[None, None, :]
    ) & served[:, :, None]
    pick = pick.astype(jnp.float32).reshape(n_shot * per_owner, tiles_dev)
    partial_sum = jnp.einsum(
        "sd,sc->dc",
        pick,
        arrived.reshape(n_shot * per_owner, 3 * tile_cells),
        precision=lax.Precision.HIGHEST,
        preferred_element_type=jnp.float32,
    )
    partial_sum = partial_sum.reshape(tiles_dev, 3, tile_cells)
    total = lax.psum(partial_sum, ("sub", "rep"))
    new_accum = accum + total * total
    new_model = model - learn_rate * total / jnp.sqrt(new_accum)
    return (new_model, new_accum)


def solution(mesh):
    in_specs = (
        P(("groups", "shot"), None, None),
        P(("groups", "shot"), None, None),
        P("groups"),
        P("groups", "sub", None),
        P(("groups", "shot"), "rep", None, None, "sub", None, None),
        P(("groups", "shot"), "rep", None, None, "sub", None, None),
        P(("groups", "shot"), "rep", None, None),
        P(("groups", "shot"), "rep", None),
        P(("groups", "shot"), "rep", None, None),
        P(("groups", "shot"), "rep", None, None, None),
    )
    out_specs = (P(("groups", "shot"), None, None), P(("groups", "shot"), None, None))
    return jax.shard_map(
        on_device, mesh=mesh, in_specs=in_specs, out_specs=out_specs, check_vma=False
    )
```

```python
import jax
import jax.numpy as jnp
from jax import lax
from jax.experimental import pallas as pl
from jax.experimental.pallas import tpu as pltpu
from jax.sharding import PartitionSpec as P

DEPTH = 32
TILE_X = 4
TILE_Y = 5
SLAB_XT = 2
SLAB_YT = 16
NSTEPS = 2
SLAB_TILES = 32
LX = SLAB_XT * TILE_X
WY = SLAB_YT * TILE_Y
LANES = 128

time_step = 0.18
learn_rate = 0.5
MESH = pl.DeviceIdType.MESH
F32 = jnp.float32
BF16 = jnp.bfloat16
TILES = 32
HALF = 8
QAC = 3 * TILE_X * DEPTH

TO_PRIOR = (2, 2, 1, 4, 1)
TO_NEXT = (4, 1, 2, 2, 2)


def next_y(f):
    return pltpu.roll(f, LANES - 1, 1)


def prior_y(f):
    return pltpu.roll(f, 1, 1)


def split3(v):
    hi = v.astype(BF16)
    rest = v - hi.astype(F32)
    mid = rest.astype(BF16)
    return hi, mid, (rest - mid.astype(F32)).astype(BF16)


def dot(x, y):
    return lax.dot_general(x, y, (((1,), (0,)), ((), ())), preferred_element_type=F32)


def dot_nt(x, y):
    return lax.dot_general(x, y, (((1,), (1,)), ((), ())), preferred_element_type=F32)


def onehot(mask):
    return jnp.where(mask, 1.0, 0.0).astype(BF16)


def iotas(rows, cols):
    return (lax.broadcasted_iota(jnp.int32, (rows, cols), 0),
            lax.broadcasted_iota(jnp.int32, (rows, cols), 1))


def physics(
    model_ref, accum_ref, own_ref, aper_ref,
    start_ref, adj_ref, wave_ref, src_ref, rec_ref, obs_ref, new_model_ref, new_accum_ref,
    F, C, W, A, B, DV, ST, CNT, OB, R0,
    send_l, send_r, recv_l, recv_r, ss_l, ss_r, rs_l, rs_r,
    par_ref, grad_ref, GT, Y, OUT, RECV, RET, PSW, RETS, ARR, TP, TW, TH, SB, TF,
    g_send, g_recv, p_send, p_recv, b_send, b_recv, x_send, x_recv, w_send, w_recv,
):
    n_sub = lax.axis_size("sub")
    n_shot = lax.axis_size("shot")
    me = lax.axis_index("sub")
    shot = lax.axis_index("shot")
    rep = lax.axis_index("rep")
    partner = {"rep": 1 - rep}
    has_l = me > 0
    has_r = me < n_sub - 1
    left = {"sub": jnp.maximum(me - 1, 0)}
    right = {"sub": jnp.minimum(me + 1, n_sub - 1)}
    barrier = pltpu.get_barrier_semaphore()
    others = [{"shot": lax.rem(shot + j, n_shot)} for j in range(1, n_shot)]
    others += [{"sub": lax.rem(me + j, n_sub)} for j in range(1, n_sub)]
    others += [partner]
    for other in others:
        pl.semaphore_signal(barrier, inc=1, device_id=other, device_id_type=MESH)

    n_slots = n_shot * TILES
    n_pos = n_shot * SLAB_TILES
    l8, l16 = max(LANES, n_shot * HALF), max(LANES, n_shot * 2 * HALF)
    r_, c_ = iotas(n_slots, own_ref.shape[1])
    perm = onehot(own_ref[...] == r_)
    r_, c_ = iotas(own_ref.shape[1], n_pos)
    named = onehot(aper_ref[...] == r_)
    at = dot(perm, named).astype(BF16)
    r_, c_ = iotas(n_slots, n_slots)
    lower = onehot((r_ // TILES == c_ // TILES) & (c_ < r_))
    r_, c_ = iotas(n_pos, l8)
    occ = dot(at, onehot(r_ // SLAB_TILES == c_ // HALF))
    rank = dot(lower, occ.astype(BF16))
    r_, c_ = iotas(n_slots, l8)
    place = (rep * HALF + c_ % HALF).astype(F32)
    GT[...] = jnp.where(rank == place, occ, 0.0)
    gt = GT[pl.ds(pl.multiple_of(shot * TILES, TILES), TILES)]
    g = gt.T[: n_shot * HALF].astype(BF16)
    gt = gt[:, : n_shot * HALF].astype(BF16)
    columns = []
    for b in range(TILE_Y):
        for k in range(3):
            columns.append(jnp.concatenate(
                [model_ref[k, :, pl.ds((a * TILE_Y + b) * DEPTH, DEPTH)] for a in range(TILE_X)],
                axis=1))
    flat = jnp.concatenate(columns, axis=1)
    outgoing = dot(jnp.concatenate([g, g, g], axis=1), jnp.concatenate(split3(flat), axis=0))
    for b in range(TILE_Y):
        OUT[:, b] = outgoing[:, b * QAC:(b + 1) * QAC].reshape(n_shot, HALF, QAC)

    pl.semaphore_wait(barrier, len(others))

    def gather(j):
        return pltpu.make_async_remote_copy(
            src_ref=OUT.at[lax.rem(shot + j, n_shot)], dst_ref=RECV.at[rep, shot],
            send_sem=g_send.at[j], recv_sem=g_recv.at[j],
            device_id={"shot": lax.rem(shot + j, n_shot)}, device_id_type=MESH)

    def gather_in(j):
        came = RECV.at[rep, lax.rem(shot + n_shot - j, n_shot)]
        return pltpu.make_async_remote_copy(
            src_ref=came, dst_ref=came, send_sem=g_send.at[j], recv_sem=g_recv.at[j],
            device_id={"shot": lax.rem(shot + j, n_shot)}, device_id_type=MESH)

    def share(j, half):
        came = RECV.at[half, lax.rem(shot + n_shot - j, n_shot)]
        return pltpu.make_async_remote_copy(
            src_ref=came, dst_ref=came, send_sem=p_send.at[j], recv_sem=p_recv.at[j],
            device_id=partner, device_id_type=MESH)

    for j in range(n_shot - 1, 0, -1):
        gather(j).start()
    RECV[rep, shot] = OUT[shot]
    share(0, rep).start()

    def copies(e):
        nl, nr = TO_PRIOR[e], TO_NEXT[e]
        to_l = pltpu.make_async_remote_copy(
            src_ref=send_l.at[e, pl.ds(0, nl)], dst_ref=recv_r.at[e, pl.ds(0, nl)],
            send_sem=ss_l.at[e], recv_sem=rs_r.at[e], device_id=left, device_id_type=MESH)
        to_r = pltpu.make_async_remote_copy(
            src_ref=send_r.at[e, pl.ds(0, nr)], dst_ref=recv_l.at[e, pl.ds(0, nr)],
            send_sem=ss_r.at[e], recv_sem=rs_l.at[e], device_id=right, device_id_type=MESH)
        return to_l, to_r

    def send(e, firsts, lasts):
        to_l, to_r = copies(e)

        @pl.when(has_l)
        def _():
            for k, (ref, i) in enumerate(firsts):
                send_l[e, k] = ref[i, 1]
            to_l.start()

        @pl.when(has_r)
        def _():
            for k, (ref, i) in enumerate(lasts):
                send_r[e, k] = ref[i, LX]
            to_r.start()

    def receive(e, firsts, lasts):
        to_l, to_r = copies(e)

        @pl.when(has_r)
        def _():
            to_r.wait_send()
            to_l.wait_recv()
            for k, (ref, i) in enumerate(firsts):
                ref[i, LX + 1] = recv_r[e, k]

        @pl.when(has_l)
        def _():
            to_l.wait_send()
            to_r.wait_recv()
            for k, (ref, i) in enumerate(lasts):
                ref[i, 0] = recv_l[e, k]

    zrow = lax.broadcasted_iota(jnp.int32, (DEPTH, LANES), 0)
    lane = lax.broadcasted_iota(jnp.int32, (DEPTH, LANES), 1)
    inside = lane < WY

    def next_z(f):
        return jnp.where(zrow == DEPTH - 1, 0.0, pltpu.roll(f, DEPTH - 1, 0))

    def prior_z(f):
        return jnp.where(zrow == 0, 0.0, pltpu.roll(f, 1, 0))

    def py(f):
        return next_y(f) - f

    def my(f):
        return f - prior_y(f)

    def pz(f):
        return next_z(f) - f

    def mz(f):
        return f - prior_z(f)

    def px(ref, i, x):
        return ref[i, x + 1] - ref[i, x]

    def mx(ref, i, x):
        return ref[i, x] - ref[i, x - 1]

    zero = jnp.zeros((DEPTH, LANES), F32)

    def strain_cot(x, c):
        lame = par_ref[0, x - 1]
        shear = par_ref[1, x - 1]
        trace = time_step * lame * (c[0] + c[1] + c[2])
        ds = time_step * shear
        W[0, x] = trace + 2.0 * ds * c[0]
        W[1, x] = trace + 2.0 * ds * c[1]
        W[2, x] = trace + 2.0 * ds * c[2]
        W[3, x] = ds * c[3]
        W[4, x] = ds * c[4]
        W[5, x] = ds * c[5]

    def edges_first(body, after):
        body(1)
        body(LX)
        after()
        lax.fori_loop(2, LX, lambda x, _: (body(x), 0)[1], 0)

    for i in range(9):
        F[i, 0] = zero
        F[i, LX + 1] = zero
    for i in range(6):
        W[i, 0] = zero
        W[i, LX + 1] = zero
    for i in range(3):
        A[i, 0] = zero
        A[i, LX + 1] = zero

    def load(x):
        for i in range(9):
            F[i, x] = zero
            F[i, x, :, pl.ds(0, WY)] = start_ref[i, x - 1].astype(F32)
            C[i, x - 1] = zero
            C[i, x - 1, :, pl.ds(0, WY)] = adj_ref[i, x - 1].astype(F32)

    def with_model(x):
        B[x - 1] = jnp.where(inside, 1.0 / jnp.where(inside, par_ref[2, x - 1], 1.0), 0.0)
        strain_cot(x, [C[3 + i, x - 1] for i in range(6)])

    e0 = ([(F, 3), (W, 0)], [(F, 6), (F, 7), (W, 3), (W, 4)])
    e1 = ([(F, 1), (F, 2)], [(F, 0)])
    e2 = ([(F, 3)], [(F, 6), (F, 7)])
    e3 = ([(F, 1), (F, 2), (A, 1), (A, 2)], [(F, 0), (A, 0)])
    e4 = ([(W, 0)], [(W, 3), (W, 4)])

    lax.fori_loop(1, LX + 1, lambda x, _: (load(x), 0)[1], 0)
    cell = rec_ref[...]
    q = cell >> 5
    rx = (q * 52429) >> 22
    ry = q - rx * WY
    rrow = (rx - me * LX) * DEPTH + (cell & (DEPTH - 1))
    nrec = rec_ref.shape[1]
    rows = lax.broadcasted_iota(jnp.int32, (LX * DEPTH, nrec), 0)
    cols = lax.broadcasted_iota(jnp.int32, (LANES, nrec), 0)
    at_row = jnp.where(rows == rrow, 1.0, 0.0).astype(F32)
    at_col = cols == ry
    dims = (((1,), (1,)), ((), ()))

    def spread(values):
        return lax.dot_general(
            at_row, jnp.where(at_col, values, 0.0), dims,
            precision=lax.Precision.HIGHEST, preferred_element_type=F32)

    CNT[...] = spread(jnp.ones((1, nrec), F32)).reshape(LX, DEPTH, LANES)
    OB[0] = spread(obs_ref[0:1]).reshape(LX, DEPTH, LANES)
    OB[1] = spread(obs_ref[1:2]).reshape(LX, DEPTH, LANES)

    r_, c_ = iotas(n_pos, l16)
    occ = dot(at, onehot(r_ // SLAB_TILES == shot))
    rank = dot(lower, occ.astype(BF16))
    r_, c_ = iotas(n_slots, l16)
    half_of = c_ // (n_shot * HALF)
    owner_of = c_ // HALF - half_of * n_shot
    place = (half_of * HALF + c_ % HALF).astype(F32)
    chunk = jnp.where((rank == place) & (owner_of == r_ // TILES), occ, 0.0)
    r_, c_ = iotas(n_pos, SLAB_XT * LANES)
    pos = r_ % SLAB_TILES
    in_y = c_ % LANES
    cover = (r_ // SLAB_TILES == shot) & (pos // SLAB_YT == c_ // LANES)
    cover = cover & (pos % SLAB_YT == in_y // TILE_Y)
    cells_of = dot(at, onehot(cover)).astype(BF16)
    where_ = dot(chunk.T.astype(BF16), cells_of)[: 2 * n_shot * HALF]
    r_, c_ = iotas(2 * n_shot * HALF, SLAB_XT * LANES)
    for b in range(TILE_Y):
        part = jnp.where(c_ % LANES % TILE_Y == b, where_, 0.0)
        Y[:, b] = part.reshape(2 * n_shot, HALF, SLAB_XT * LANES)
    k_rows = 2 * n_shot * TILE_Y * HALF
    ymat = Y[...].reshape(k_rows, SLAB_XT * LANES).astype(BF16)

    for j in range(1, n_shot):
        gather_in(j).wait_recv()
        share(j, rep).start()
    for j in range(n_shot):
        share(j, 1 - rep).wait_recv()
    came = RECV[...].reshape(k_rows, QAC).T
    slab = None
    for piece in split3(came):
        term = dot(piece, ymat)
        slab = term if slab is None else slab + term
    for k in range(3):
        for a in range(TILE_X):
            for i in range(SLAB_XT):
                par_ref[k, i * TILE_X + a] = slab[
                    (k * TILE_X + a) * DEPTH:(k * TILE_X + a + 1) * DEPTH,
                    i * LANES:(i + 1) * LANES]
    edges_first(with_model, lambda: send(0, *e0))

    scell = src_ref[0]
    sq = scell >> 5
    sx = (sq * 52429) >> 22
    sy = sq - sx * WY
    sz = scell & (DEPTH - 1)
    at_src = jnp.where((zrow == sz) & (lane == sy), 1.0, 0.0)

    def divergence(x):
        return [
            px(F, 3, x) + my(F[6, x]) + mz(F[7, x]),
            mx(F, 6, x) + py(F[4, x]) + mz(F[8, x]),
            mx(F, 7, x) + my(F[8, x]) + pz(F[5, x]),
        ]

    def strains(x):
        vx, vy, vz = F[0, x], F[1, x], F[2, x]
        return [
            mx(F, 0, x), my(vy), mz(vz),
            py(vx) + px(F, 1, x), pz(vx) + px(F, 2, x), pz(vy) + py(vz),
        ]

    def velocity_cot(x):
        exx, eyy, ezz = W[0, x], W[1, x], W[2, x]
        gxy, gxz, gyz = W[3, x], W[4, x], W[5, x]
        return [
            px(W, 0, x) + my(gxy) + mz(gxz),
            py(eyy) + mx(W, 3, x) + mz(gyz),
            pz(ezz) + mx(W, 4, x) + my(gyz),
        ]

    def first_velocity(x):
        b = time_step * B[x - 1]
        d = divergence(x)
        for i in range(3):
            DV[i, x - 1] = d[i]
            F[i, x] = F[i, x] + b * d[i]
        R0[x - 1] = CNT[x - 1] * F[2, x] - OB[0, x - 1]

    receive(0, *e0)
    edges_first(first_velocity, lambda: send(1, *e1))

    def first_stress(x):
        lame = time_step * par_ref[0, x - 1]
        shear = time_step * par_ref[1, x - 1]
        s = strains(x)
        for i in range(6):
            ST[i, x - 1] = s[i]
        amp = jnp.where(x - 1 + me * LX == sx, time_step * wave_ref[0], 0.0)
        base = lame * (s[0] + s[1] + s[2]) + amp * at_src
        for i in range(3):
            F[3 + i, x] = F[3 + i, x] + (base + 2.0 * shear * s[i])
            F[6 + i, x] = F[6 + i, x] + shear * s[3 + i]

    receive(1, *e1)
    edges_first(first_stress, lambda: send(2, *e2))

    def second_velocity(x):
        inv = B[x - 1]
        b = time_step * inv
        d = divergence(x)
        w = velocity_cot(x)
        for i in range(3):
            F[i, x] = F[i, x] + b * d[i]
        res = CNT[x - 1] * F[2, x] - OB[1, x - 1]
        total = zero
        for i in range(3):
            c = C[i, x - 1] - w[i]
            if i == 2:
                c = c + res
            C[i, x - 1] = c
            a = b * c
            A[i, x] = a
            total = total + a * d[i]
        grad_ref[2, x - 1] = -inv * total

    receive(2, *e2)
    edges_first(second_velocity, lambda: send(3, *e3))

    def model_part(c, s):
        part_lame = (s[0] + s[1] + s[2]) * (c[0] + c[1] + c[2])
        part_shear = 2.0 * (s[0] * c[0] + s[1] * c[1] + s[2] * c[2]) + (
            s[3] * c[3] + s[4] * c[4] + s[5] * c[5])
        return part_lame, part_shear

    def stress_back(x):
        c = [C[3 + i, x - 1] for i in range(6)]
        lame1, shear1 = model_part(c, strains(x))
        ax, ay, az = A[0, x], A[1, x], A[2, x]
        c = [
            c[0] - mx(A, 0, x),
            c[1] - my(ay),
            c[2] - mz(az),
            c[3] - py(ax) - px(A, 1, x),
            c[4] - pz(ax) - px(A, 2, x),
            c[5] - pz(ay) - py(az),
        ]
        strain_cot(x, c)
        lame0, shear0 = model_part(c, [ST[i, x - 1] for i in range(6)])
        grad_ref[0, x - 1] = time_step * (lame1 + lame0)
        grad_ref[1, x - 1] = time_step * (shear1 + shear0)

    receive(3, *e3)
    edges_first(stress_back, lambda: send(4, *e4))

    def last_velocity(x):
        inv = B[x - 1]
        b = time_step * inv
        w = velocity_cot(x)
        total = zero
        for i in range(3):
            c = C[i, x - 1] - w[i]
            if i == 2:
                c = c + R0[x - 1]
            total = total + b * c * DV[i, x - 1]
        grad_ref[2, x - 1] = grad_ref[2, x - 1] - inv * total

    receive(4, *e4)
    lax.fori_loop(1, LX + 1, lambda x, _: (last_velocity(x), 0)[1], 0)


    rows_ = []
    for k in range(3):
        for a in range(TILE_X):
            rows_.append(jnp.concatenate(
                [grad_ref[k, i * TILE_X + a] for i in range(SLAB_XT)], axis=1))
    rows_ = jnp.concatenate(rows_, axis=0)
    back = None
    for piece in split3(rows_):
        term = dot_nt(ymat, piece)
        back = term if back is None else back + term
    RET[...] = back.reshape(2, n_shot, TILE_Y, HALF, QAC)

    def swap(src, dst, k):
        return pltpu.make_async_remote_copy(
            src_ref=src, dst_ref=dst, send_sem=w_send.at[k], recv_sem=w_recv.at[k],
            device_id=partner, device_id_type=MESH)

    for j in range(n_shot):
        o = lax.rem(shot + n_shot - j, n_shot)
        swap(RET.at[1 - rep, o], PSW.at[o], j).start()

    def give(j):
        return pltpu.make_async_remote_copy(
            src_ref=RETS.at[lax.rem(shot + n_shot - j, n_shot)], dst_ref=ARR.at[shot],
            send_sem=b_send.at[j], recv_sem=b_recv.at[j],
            device_id={"shot": lax.rem(shot + n_shot - j, n_shot)}, device_id_type=MESH)

    def give_in(j):
        o = lax.rem(shot + j, n_shot)
        return pltpu.make_async_remote_copy(
            src_ref=ARR.at[o], dst_ref=ARR.at[o], send_sem=b_send.at[j],
            recv_sem=b_recv.at[j], device_id={"shot": o}, device_id_type=MESH)

    for j in list(range(1, n_shot)) + [0]:
        o = lax.rem(shot + n_shot - j, n_shot)
        swap(RET.at[1 - rep, o], PSW.at[o], j).wait_recv()
        if j > 0:
            RETS[o] = RET[rep, o] + PSW[o]
            give(j).start()
        else:
            ARR[o] = RET[rep, o] + PSW[o]
    for j in range(1, n_shot):
        give_in(j).wait_recv()
    ggg = jnp.concatenate([gt, gt, gt], axis=1)
    half_rows = TILES // 2
    for b in range(TILE_Y):
        arrived = ARR[:, b].reshape(n_shot * HALF, QAC)
        part = dot(ggg, jnp.concatenate(split3(arrived), axis=0))
        TP[0, b] = part[:half_rows]
        TP[1, b] = part[half_rows:]

    first = swap(TP.at[1 - rep], TW, n_shot)
    first.start()
    first.wait()
    SB[me] = TP[rep] + TW[...]

    def across(j):
        return pltpu.make_async_remote_copy(
            src_ref=SB.at[me], dst_ref=SB.at[me], send_sem=x_send.at[j], recv_sem=x_recv.at[j],
            device_id={"sub": lax.rem(me + j, n_sub)}, device_id_type=MESH)

    def across_in(j):
        u = lax.rem(me + n_sub - j, n_sub)
        return pltpu.make_async_remote_copy(
            src_ref=SB.at[u], dst_ref=SB.at[u], send_sem=x_send.at[j], recv_sem=x_recv.at[j],
            device_id={"sub": lax.rem(me + j, n_sub)}, device_id_type=MESH)

    for j in range(1, n_sub):
        across(j).start()
    for j in range(1, n_sub):
        across_in(j).wait_recv()
    total = SB[0]
    for u in range(1, n_sub):
        total = total + SB[u]
    TF[rep] = total
    TH[...] = total
    last = swap(TH, TF.at[rep], n_shot + 1)
    last.start()
    pltpu.make_async_remote_copy(
        src_ref=TH, dst_ref=TF.at[1 - rep], send_sem=w_send.at[n_shot + 1],
        recv_sem=w_recv.at[n_shot + 1], device_id=partner, device_id_type=MESH).wait_recv()

    for k in range(3):
        for h in range(2):
            grad = jnp.concatenate(
                [TF[h, b, :, pl.ds((k * TILE_X + a) * DEPTH, DEPTH)]
                 for a in range(TILE_X) for b in range(TILE_Y)], axis=1)
            rows = pl.ds(h * half_rows, half_rows)
            new_accum = accum_ref[k, rows] + grad * grad
            new_accum_ref[k, rows] = new_accum
            new_model_ref[k, rows] = model_ref[k, rows] - learn_rate * grad / jnp.sqrt(new_accum)

    last.wait_send()
    for j in range(1, n_shot):
        gather(j).wait_send()
        give(j).wait_send()
    for j in range(n_shot):
        o = lax.rem(shot + n_shot - j, n_shot)
        share(j, rep).wait_send()
        swap(RET.at[1 - rep, o], PSW.at[o], j).wait_send()
    for j in range(1, n_sub):
        across(j).wait_send()


def run_window(model, accum, own, aper, start, adj, wave, src, rec, obs):
    n_shot = lax.axis_size("shot")
    n_sub = lax.axis_size("sub")
    vm = pl.BlockSpec(memory_space=pltpu.VMEM)
    sm = pl.BlockSpec(memory_space=pltpu.SMEM)
    layer = (DEPTH, LANES)
    half = TILES // 2
    dma = pltpu.SemaphoreType.DMA
    halo = pltpu.VMEM((5, 4) + layer, F32)
    rim = dma((5,))

    def vmem(*shape):
        return pltpu.VMEM(shape, F32)

    chunk = (TILE_Y, HALF, QAC)
    return pl.pallas_call(
        physics,
        out_shape=[jax.ShapeDtypeStruct(model.shape, F32)] * 2,
        in_specs=[vm, vm, vm, vm, vm, vm, sm, sm, vm, vm],
        out_specs=[vm, vm],
        scratch_shapes=[
            vmem(9, LX + 2, *layer), vmem(9, LX, *layer), vmem(6, LX + 2, *layer),
            vmem(3, LX + 2, *layer), vmem(LX, *layer), vmem(3, LX, *layer),
            vmem(6, LX, *layer), vmem(LX, *layer), vmem(2, LX, *layer), vmem(LX, *layer),
            halo, halo, halo, halo, rim, rim, rim, rim,
            vmem(3, LX, *layer), vmem(3, LX, *layer),
            vmem(n_shot * TILES, max(LANES, n_shot * HALF)),
            vmem(2 * n_shot, TILE_Y, HALF, SLAB_XT * LANES),
            vmem(n_shot, *chunk), vmem(2, n_shot, *chunk), vmem(2, n_shot, *chunk),
            vmem(n_shot, *chunk), vmem(n_shot, *chunk), vmem(n_shot, *chunk),
            vmem(2, TILE_Y, half, QAC), vmem(TILE_Y, half, QAC), vmem(TILE_Y, half, QAC),
            vmem(n_sub, TILE_Y, half, QAC), vmem(2, TILE_Y, half, QAC),
            dma((n_shot,)), dma((n_shot,)), dma((n_shot,)), dma((n_shot,)),
            dma((n_shot,)), dma((n_shot,)), dma((n_sub,)), dma((n_sub,)),
            dma((n_shot + 2,)), dma((n_shot + 2,)),
        ],
        compiler_params=pltpu.CompilerParams(
            collective_id=0, has_side_effects=True, vmem_limit_bytes=52 * 1024 * 1024),
    )(model, accum, own, aper, start, adj, wave, src, rec, obs)


def on_device(
    model, accum, owner_map, aperture, start_state, adjoint_end, wavelet, source_cell,
    receiver_cell, observed,
):
    start = start_state[0, 0, 0].transpose(0, 1, 3, 2)
    adj = adjoint_end[0, 0, 0].transpose(0, 1, 3, 2)
    new_model, new_accum = run_window(
        model.transpose(1, 0, 2), accum.transpose(1, 0, 2), owner_map.reshape(1, -1),
        aperture.reshape(1, -1), start, adj, wavelet.reshape(NSTEPS), source_cell.reshape(1),
        receiver_cell.reshape(1, -1), observed[0, 0, 0],
    )
    return (new_model.transpose(1, 0, 2), new_accum.transpose(1, 0, 2))


def solution(mesh):
    in_specs = (
        P(("groups", "shot"), None, None),
        P(("groups", "shot"), None, None),
        P("groups"),
        P("groups", "sub", None),
        P(("groups", "shot"), "rep", None, None, "sub", None, None),
        P(("groups", "shot"), "rep", None, None, "sub", None, None),
        P(("groups", "shot"), "rep", None, None),
        P(("groups", "shot"), "rep", None),
        P(("groups", "shot"), "rep", None, None),
        P(("groups", "shot"), "rep", None, None, None),
    )
    out_specs = (P(("groups", "shot"), None, None), P(("groups", "shot"), None, None))
    return jax.shard_map(
        on_device, mesh=mesh, in_specs=in_specs, out_specs=out_specs, check_vma=False
    )
```

```python
import jax
import jax.numpy as jnp
from jax import lax
from jax.experimental import pallas as pl
from jax.experimental.pallas import tpu as pltpu
from jax.sharding import PartitionSpec as P

DEPTH = 32
TILE_X = 4
TILE_Y = 5
SLAB_XT = 2
SLAB_YT = 16
NSTEPS = 2
SLAB_TILES = 32
LX = SLAB_XT * TILE_X
WY = SLAB_YT * TILE_Y
LANES = 128

time_step = 0.18
learn_rate = 0.5
MESH = pl.DeviceIdType.MESH
F32 = jnp.float32
BF16 = jnp.bfloat16
TILES = 32
HALF = 8
QAC = 3 * TILE_X * DEPTH

TO_PRIOR = (2, 2, 1, 4, 1)
TO_NEXT = (4, 1, 2, 2, 2)


def next_y(f):
    return pltpu.roll(f, LANES - 1, 1)


def prior_y(f):
    return pltpu.roll(f, 1, 1)


def split3(v):
    hi = v.astype(BF16)
    rest = v - hi.astype(F32)
    mid = rest.astype(BF16)
    return hi, mid, (rest - mid.astype(F32)).astype(BF16)


def dot(x, y):
    return lax.dot_general(x, y, (((1,), (0,)), ((), ())), preferred_element_type=F32)


def dot_nt(x, y):
    return lax.dot_general(x, y, (((1,), (1,)), ((), ())), preferred_element_type=F32)


def onehot(mask):
    return jnp.where(mask, 1.0, 0.0).astype(BF16)


def iotas(rows, cols):
    return (lax.broadcasted_iota(jnp.int32, (rows, cols), 0),
            lax.broadcasted_iota(jnp.int32, (rows, cols), 1))


def physics(
    model_hbm, accum_hbm, own_ref, aper_ref,
    start_hbm, adj_hbm, wave_ref, src_ref, rec_ref, obs_ref, new_model_ref, new_accum_ref,
    F, C, W, A, B, DV, ST, CNT, OB, R0,
    send_l, send_r, recv_l, recv_r, ss_l, ss_r, rs_l, rs_r,
    par_ref, grad_ref, GT, Y, OUT, RECV, RET, PSW, RETS, ARR, TP, TW, TH, SB, TF,
    g_send, g_recv, p_send, p_recv, b_send, b_recv, x_send, x_recv, w_send, w_recv,
    model_ref, accum_ref, start_ref, adj_ref, l_sem, v_send, v_recv, y_send, y_recv,
):
    fetch = [
        pltpu.make_async_copy(src, dst, l_sem.at[i])
        for i, (src, dst) in enumerate([
            (model_hbm, model_ref), (start_hbm, start_ref), (adj_hbm, adj_ref),
            (accum_hbm, accum_ref)])
    ]
    for copy in fetch:
        copy.start()
    n_sub = lax.axis_size("sub")
    n_shot = lax.axis_size("shot")
    me = lax.axis_index("sub")
    shot = lax.axis_index("shot")
    rep = lax.axis_index("rep")
    partner = {"rep": 1 - rep}
    has_l = me > 0
    has_r = me < n_sub - 1
    left = {"sub": jnp.maximum(me - 1, 0)}
    right = {"sub": jnp.minimum(me + 1, n_sub - 1)}
    barrier = pltpu.get_barrier_semaphore()
    others = [{"shot": lax.rem(shot + j, n_shot)} for j in range(1, n_shot)]
    others += [{"sub": lax.rem(me + j, n_sub)} for j in range(1, n_sub)]
    others += [partner]
    for other in others:
        pl.semaphore_signal(barrier, inc=1, device_id=other, device_id_type=MESH)

    n_slots = n_shot * TILES
    n_pos = n_shot * SLAB_TILES
    l8, l16 = max(LANES, n_shot * HALF), max(LANES, n_shot * 2 * HALF)
    r_, c_ = iotas(n_slots, own_ref.shape[1])
    perm = onehot(own_ref[...] == r_)
    r_, c_ = iotas(own_ref.shape[1], n_pos)
    ids = jnp.concatenate([aper_ref[s] for s in range(n_shot)], axis=1)
    named = onehot(ids == r_)
    at = dot(perm, named).astype(BF16)
    r_, c_ = iotas(n_slots, n_slots)
    lower = onehot((r_ // TILES == c_ // TILES) & (c_ < r_))
    r_, c_ = iotas(n_pos, l8)
    occ = dot(at, onehot(r_ // SLAB_TILES == c_ // HALF))
    rank = dot(lower, occ.astype(BF16))
    r_, c_ = iotas(n_slots, l8)
    place = (rep * HALF + c_ % HALF).astype(F32)
    GT[...] = jnp.where(rank == place, occ, 0.0)
    gt = GT[pl.ds(pl.multiple_of(shot * TILES, TILES), TILES)]
    g = gt.T[: n_shot * HALF].astype(BF16)
    gt = gt[:, : n_shot * HALF].astype(BF16)
    fetch[0].wait()
    columns = []
    for b in range(TILE_Y):
        for k in range(3):
            columns.append(jnp.concatenate(
                [model_ref[k, :, pl.ds((a * TILE_Y + b) * DEPTH, DEPTH)] for a in range(TILE_X)],
                axis=1))
    flat = jnp.concatenate(columns, axis=1)
    outgoing = dot(jnp.concatenate([g, g, g], axis=1), jnp.concatenate(split3(flat), axis=0))
    for b in range(TILE_Y):
        OUT[:, b] = outgoing[:, b * QAC:(b + 1) * QAC].reshape(n_shot, HALF, QAC)

    pl.semaphore_wait(barrier, len(others))

    def gather(j):
        return pltpu.make_async_remote_copy(
            src_ref=OUT.at[lax.rem(shot + j, n_shot)], dst_ref=RECV.at[rep, shot],
            send_sem=g_send.at[j], recv_sem=g_recv.at[j],
            device_id={"shot": lax.rem(shot + j, n_shot)}, device_id_type=MESH)

    def gather_in(j):
        came = RECV.at[rep, lax.rem(shot + n_shot - j, n_shot)]
        return pltpu.make_async_remote_copy(
            src_ref=came, dst_ref=came, send_sem=g_send.at[j], recv_sem=g_recv.at[j],
            device_id={"shot": lax.rem(shot + j, n_shot)}, device_id_type=MESH)

    def share(j, half):
        came = RECV.at[half, lax.rem(shot + n_shot - j, n_shot)]
        return pltpu.make_async_remote_copy(
            src_ref=came, dst_ref=came, send_sem=p_send.at[j], recv_sem=p_recv.at[j],
            device_id=partner, device_id_type=MESH)

    for j in range(n_shot - 1, 0, -1):
        gather(j).start()
    RECV[rep, shot] = OUT[shot]
    share(0, rep).start()

    def copies(e):
        nl, nr = TO_PRIOR[e], TO_NEXT[e]
        to_l = pltpu.make_async_remote_copy(
            src_ref=send_l.at[e, pl.ds(0, nl)], dst_ref=recv_r.at[e, pl.ds(0, nl)],
            send_sem=ss_l.at[e], recv_sem=rs_r.at[e], device_id=left, device_id_type=MESH)
        to_r = pltpu.make_async_remote_copy(
            src_ref=send_r.at[e, pl.ds(0, nr)], dst_ref=recv_l.at[e, pl.ds(0, nr)],
            send_sem=ss_r.at[e], recv_sem=rs_l.at[e], device_id=right, device_id_type=MESH)
        return to_l, to_r

    def send(e, firsts, lasts):
        to_l, to_r = copies(e)

        @pl.when(has_l)
        def _():
            for k, (ref, i) in enumerate(firsts):
                send_l[e, k] = ref[i, 1]
            to_l.start()

        @pl.when(has_r)
        def _():
            for k, (ref, i) in enumerate(lasts):
                send_r[e, k] = ref[i, LX]
            to_r.start()

    def receive(e, firsts, lasts):
        to_l, to_r = copies(e)

        @pl.when(has_r)
        def _():
            to_r.wait_send()
            to_l.wait_recv()
            for k, (ref, i) in enumerate(firsts):
                ref[i, LX + 1] = recv_r[e, k]

        @pl.when(has_l)
        def _():
            to_l.wait_send()
            to_r.wait_recv()
            for k, (ref, i) in enumerate(lasts):
                ref[i, 0] = recv_l[e, k]

    zrow = lax.broadcasted_iota(jnp.int32, (DEPTH, LANES), 0)
    lane = lax.broadcasted_iota(jnp.int32, (DEPTH, LANES), 1)
    inside = lane < WY

    def next_z(f):
        return jnp.where(zrow == DEPTH - 1, 0.0, pltpu.roll(f, DEPTH - 1, 0))

    def prior_z(f):
        return jnp.where(zrow == 0, 0.0, pltpu.roll(f, 1, 0))

    def py(f):
        return next_y(f) - f

    def my(f):
        return f - prior_y(f)

    def pz(f):
        return next_z(f) - f

    def mz(f):
        return f - prior_z(f)

    def px(ref, i, x):
        return ref[i, x + 1] - ref[i, x]

    def mx(ref, i, x):
        return ref[i, x] - ref[i, x - 1]

    zero = jnp.zeros((DEPTH, LANES), F32)

    def strain_cot(x, c):
        lame = par_ref[0, x - 1]
        shear = par_ref[1, x - 1]
        trace = time_step * lame * (c[0] + c[1] + c[2])
        ds = time_step * shear
        W[0, x] = trace + 2.0 * ds * c[0]
        W[1, x] = trace + 2.0 * ds * c[1]
        W[2, x] = trace + 2.0 * ds * c[2]
        W[3, x] = ds * c[3]
        W[4, x] = ds * c[4]
        W[5, x] = ds * c[5]

    def edges_first(body, after):
        body(1)
        body(LX)
        after()
        lax.fori_loop(2, LX, lambda x, _: (body(x), 0)[1], 0)

    for i in range(9):
        F[i, 0] = zero
        F[i, LX + 1] = zero
    for i in range(6):
        W[i, 0] = zero
        W[i, LX + 1] = zero
    for i in range(3):
        A[i, 0] = zero
        A[i, LX + 1] = zero

    def load(x):
        for i in range(9):
            F[i, x] = zero
            F[i, x, :, pl.ds(0, WY)] = start_ref[i, x - 1].astype(F32)
            C[i, x - 1] = zero
            C[i, x - 1, :, pl.ds(0, WY)] = adj_ref[i, x - 1].astype(F32)

    def with_model(x):
        B[x - 1] = jnp.where(inside, 1.0 / jnp.where(inside, par_ref[2, x - 1], 1.0), 0.0)
        strain_cot(x, [C[3 + i, x - 1] for i in range(6)])

    e0 = ([(F, 3), (W, 0)], [(F, 6), (F, 7), (W, 3), (W, 4)])
    e1 = ([(F, 1), (F, 2)], [(F, 0)])
    e2 = ([(F, 3)], [(F, 6), (F, 7)])
    e3 = ([(F, 1), (F, 2), (A, 1), (A, 2)], [(F, 0), (A, 0)])
    e4 = ([(W, 0)], [(W, 3), (W, 4)])

    fetch[1].wait()
    fetch[2].wait()
    lax.fori_loop(1, LX + 1, lambda x, _: (load(x), 0)[1], 0)
    cell = rec_ref[...]
    q = cell >> 5
    rx = (q * 52429) >> 22
    ry = q - rx * WY
    rrow = (rx - me * LX) * DEPTH + (cell & (DEPTH - 1))
    nrec = rec_ref.shape[1]
    rows = lax.broadcasted_iota(jnp.int32, (LX * DEPTH, nrec), 0)
    cols = lax.broadcasted_iota(jnp.int32, (LANES, nrec), 0)
    at_row = jnp.where(rows == rrow, 1.0, 0.0).astype(F32)
    at_col = cols == ry
    dims = (((1,), (1,)), ((), ()))

    def spread(values):
        return lax.dot_general(
            at_row, jnp.where(at_col, values, 0.0), dims,
            precision=lax.Precision.HIGHEST, preferred_element_type=F32)

    CNT[...] = spread(jnp.ones((1, nrec), F32)).reshape(LX, DEPTH, LANES)
    OB[0] = spread(obs_ref[0:1]).reshape(LX, DEPTH, LANES)
    OB[1] = spread(obs_ref[1:2]).reshape(LX, DEPTH, LANES)

    r_, c_ = iotas(n_pos, l16)
    occ = dot(at, onehot(r_ // SLAB_TILES == shot))
    rank = dot(lower, occ.astype(BF16))
    r_, c_ = iotas(n_slots, l16)
    half_of = c_ // (n_shot * HALF)
    owner_of = c_ // HALF - half_of * n_shot
    place = (half_of * HALF + c_ % HALF).astype(F32)
    chunk = jnp.where((rank == place) & (owner_of == r_ // TILES), occ, 0.0)
    r_, c_ = iotas(n_pos, SLAB_XT * LANES)
    pos = r_ % SLAB_TILES
    in_y = c_ % LANES
    cover = (r_ // SLAB_TILES == shot) & (pos // SLAB_YT == c_ // LANES)
    cover = cover & (pos % SLAB_YT == in_y // TILE_Y)
    cells_of = dot(at, onehot(cover)).astype(BF16)
    where_ = dot(chunk.T.astype(BF16), cells_of)[: 2 * n_shot * HALF]
    r_, c_ = iotas(2 * n_shot * HALF, SLAB_XT * LANES)
    for b in range(TILE_Y):
        part = jnp.where(c_ % LANES % TILE_Y == b, where_, 0.0)
        Y[:, b] = part.reshape(2 * n_shot, HALF, SLAB_XT * LANES)
    k_rows = 2 * n_shot * TILE_Y * HALF
    ymat = Y[...].reshape(k_rows, SLAB_XT * LANES).astype(BF16)

    for j in range(1, n_shot):
        gather_in(j).wait_recv()
        share(j, rep).start()
    for j in range(n_shot):
        share(j, 1 - rep).wait_recv()
    came = RECV[...].reshape(k_rows, QAC).T
    slab = None
    for piece in split3(came):
        term = dot(piece, ymat)
        slab = term if slab is None else slab + term
    for k in range(3):
        for a in range(TILE_X):
            for i in range(SLAB_XT):
                par_ref[k, i * TILE_X + a] = slab[
                    (k * TILE_X + a) * DEPTH:(k * TILE_X + a + 1) * DEPTH,
                    i * LANES:(i + 1) * LANES]
    edges_first(with_model, lambda: send(0, *e0))

    scell = src_ref[0]
    sq = scell >> 5
    sx = (sq * 52429) >> 22
    sy = sq - sx * WY
    sz = scell & (DEPTH - 1)
    at_src = jnp.where((zrow == sz) & (lane == sy), 1.0, 0.0)

    def divergence(x):
        return [
            px(F, 3, x) + my(F[6, x]) + mz(F[7, x]),
            mx(F, 6, x) + py(F[4, x]) + mz(F[8, x]),
            mx(F, 7, x) + my(F[8, x]) + pz(F[5, x]),
        ]

    def strains(x):
        vx, vy, vz = F[0, x], F[1, x], F[2, x]
        return [
            mx(F, 0, x), my(vy), mz(vz),
            py(vx) + px(F, 1, x), pz(vx) + px(F, 2, x), pz(vy) + py(vz),
        ]

    def velocity_cot(x):
        exx, eyy, ezz = W[0, x], W[1, x], W[2, x]
        gxy, gxz, gyz = W[3, x], W[4, x], W[5, x]
        return [
            px(W, 0, x) + my(gxy) + mz(gxz),
            py(eyy) + mx(W, 3, x) + mz(gyz),
            pz(ezz) + mx(W, 4, x) + my(gyz),
        ]

    def first_velocity(x):
        b = time_step * B[x - 1]
        d = divergence(x)
        for i in range(3):
            DV[i, x - 1] = d[i]
            F[i, x] = F[i, x] + b * d[i]
        R0[x - 1] = CNT[x - 1] * F[2, x] - OB[0, x - 1]

    receive(0, *e0)
    edges_first(first_velocity, lambda: send(1, *e1))

    def first_stress(x):
        lame = time_step * par_ref[0, x - 1]
        shear = time_step * par_ref[1, x - 1]
        s = strains(x)
        for i in range(6):
            ST[i, x - 1] = s[i]
        amp = jnp.where(x - 1 + me * LX == sx, time_step * wave_ref[0], 0.0)
        base = lame * (s[0] + s[1] + s[2]) + amp * at_src
        for i in range(3):
            F[3 + i, x] = F[3 + i, x] + (base + 2.0 * shear * s[i])
            F[6 + i, x] = F[6 + i, x] + shear * s[3 + i]

    receive(1, *e1)
    edges_first(first_stress, lambda: send(2, *e2))

    def second_velocity(x):
        inv = B[x - 1]
        b = time_step * inv
        d = divergence(x)
        w = velocity_cot(x)
        for i in range(3):
            F[i, x] = F[i, x] + b * d[i]
        res = CNT[x - 1] * F[2, x] - OB[1, x - 1]
        total = zero
        for i in range(3):
            c = C[i, x - 1] - w[i]
            if i == 2:
                c = c + res
            C[i, x - 1] = c
            a = b * c
            A[i, x] = a
            total = total + a * d[i]
        grad_ref[2, x - 1] = -inv * total

    receive(2, *e2)
    edges_first(second_velocity, lambda: send(3, *e3))

    def model_part(c, s):
        part_lame = (s[0] + s[1] + s[2]) * (c[0] + c[1] + c[2])
        part_shear = 2.0 * (s[0] * c[0] + s[1] * c[1] + s[2] * c[2]) + (
            s[3] * c[3] + s[4] * c[4] + s[5] * c[5])
        return part_lame, part_shear

    def stress_back(x):
        c = [C[3 + i, x - 1] for i in range(6)]
        lame1, shear1 = model_part(c, strains(x))
        ax, ay, az = A[0, x], A[1, x], A[2, x]
        c = [
            c[0] - mx(A, 0, x),
            c[1] - my(ay),
            c[2] - mz(az),
            c[3] - py(ax) - px(A, 1, x),
            c[4] - pz(ax) - px(A, 2, x),
            c[5] - pz(ay) - py(az),
        ]
        strain_cot(x, c)
        lame0, shear0 = model_part(c, [ST[i, x - 1] for i in range(6)])
        grad_ref[0, x - 1] = time_step * (lame1 + lame0)
        grad_ref[1, x - 1] = time_step * (shear1 + shear0)

    receive(3, *e3)
    edges_first(stress_back, lambda: send(4, *e4))

    def last_velocity(x):
        inv = B[x - 1]
        b = time_step * inv
        w = velocity_cot(x)
        total = zero
        for i in range(3):
            c = C[i, x - 1] - w[i]
            if i == 2:
                c = c + R0[x - 1]
            total = total + b * c * DV[i, x - 1]
        grad_ref[2, x - 1] = grad_ref[2, x - 1] - inv * total

    receive(4, *e4)
    lax.fori_loop(1, LX + 1, lambda x, _: (last_velocity(x), 0)[1], 0)


    rows_ = []
    for k in range(3):
        for a in range(TILE_X):
            rows_.append(jnp.concatenate(
                [grad_ref[k, i * TILE_X + a] for i in range(SLAB_XT)], axis=1))
    rows_ = jnp.concatenate(rows_, axis=0)
    back = None
    for piece in split3(rows_):
        term = dot_nt(ymat, piece)
        back = term if back is None else back + term
    RET[...] = back.reshape(2, n_shot, TILE_Y, HALF, QAC)

    def swap(src, dst, k):
        return pltpu.make_async_remote_copy(
            src_ref=src, dst_ref=dst, send_sem=w_send.at[k], recv_sem=w_recv.at[k],
            device_id=partner, device_id_type=MESH)

    for j in range(n_shot):
        o = lax.rem(shot + n_shot - j, n_shot)
        swap(RET.at[1 - rep, o], PSW.at[o], j).start()

    def give(j):
        return pltpu.make_async_remote_copy(
            src_ref=RETS.at[lax.rem(shot + n_shot - j, n_shot)], dst_ref=ARR.at[shot],
            send_sem=b_send.at[j], recv_sem=b_recv.at[j],
            device_id={"shot": lax.rem(shot + n_shot - j, n_shot)}, device_id_type=MESH)

    def give_in(j):
        o = lax.rem(shot + j, n_shot)
        return pltpu.make_async_remote_copy(
            src_ref=ARR.at[o], dst_ref=ARR.at[o], send_sem=b_send.at[j],
            recv_sem=b_recv.at[j], device_id={"shot": o}, device_id_type=MESH)

    for j in list(range(1, n_shot)) + [0]:
        o = lax.rem(shot + n_shot - j, n_shot)
        swap(RET.at[1 - rep, o], PSW.at[o], j).wait_recv()
        if j > 0:
            RETS[o] = RET[rep, o] + PSW[o]
            give(j).start()
        else:
            ARR[o] = RET[rep, o] + PSW[o]
    for j in range(1, n_shot):
        give_in(j).wait_recv()
    ggg = jnp.concatenate([gt, gt, gt], axis=1)
    half_rows = TILES // 2

    def to_core(b):
        return pltpu.make_async_remote_copy(
            src_ref=TP.at[1 - rep, b], dst_ref=TW.at[b], send_sem=v_send.at[b],
            recv_sem=v_recv.at[b], device_id=partner, device_id_type=MESH)

    def across(j, b):
        return pltpu.make_async_remote_copy(
            src_ref=SB.at[me, b], dst_ref=SB.at[me, b], send_sem=x_send.at[j, b],
            recv_sem=x_recv.at[j, b], device_id={"sub": lax.rem(me + j, n_sub)},
            device_id_type=MESH)

    def across_in(j, b):
        u = lax.rem(me + n_sub - j, n_sub)
        return pltpu.make_async_remote_copy(
            src_ref=SB.at[u, b], dst_ref=SB.at[u, b], send_sem=x_send.at[j, b],
            recv_sem=x_recv.at[j, b], device_id={"sub": lax.rem(me + j, n_sub)},
            device_id_type=MESH)

    def last(b, half):
        return pltpu.make_async_remote_copy(
            src_ref=TH.at[b], dst_ref=TF.at[half, b], send_sem=y_send.at[b],
            recv_sem=y_recv.at[b], device_id=partner, device_id_type=MESH)

    for b in range(TILE_Y):
        arrived = ARR[:, b].reshape(n_shot * HALF, QAC)
        part = dot(ggg, jnp.concatenate(split3(arrived), axis=0))
        TP[0, b] = part[:half_rows]
        TP[1, b] = part[half_rows:]
        to_core(b).start()
    for b in range(TILE_Y):
        to_core(b).wait_recv()
        SB[me, b] = TP[rep, b] + TW[b]
        for j in range(1, n_sub):
            across(j, b).start()
    for b in range(TILE_Y):
        for j in range(1, n_sub):
            across_in(j, b).wait_recv()
        total = SB[0, b]
        for u in range(1, n_sub):
            total = total + SB[u, b]
        TF[rep, b] = total
        TH[b] = total
        last(b, rep).start()
    fetch[3].wait()
    for b in range(TILE_Y):
        last(b, 1 - rep).wait_recv()

    for k in range(3):
        for h in range(2):
            grad = jnp.concatenate(
                [TF[h, b, :, pl.ds((k * TILE_X + a) * DEPTH, DEPTH)]
                 for a in range(TILE_X) for b in range(TILE_Y)], axis=1)
            rows = pl.ds(h * half_rows, half_rows)
            new_accum = accum_ref[k, rows] + grad * grad
            new_accum_ref[k, rows] = new_accum
            new_model_ref[k, rows] = model_ref[k, rows] - learn_rate * grad / jnp.sqrt(new_accum)

    for b in range(TILE_Y):
        last(b, rep).wait_send()
        to_core(b).wait_send()
        for j in range(1, n_sub):
            across(j, b).wait_send()
    for j in range(1, n_shot):
        gather(j).wait_send()
        give(j).wait_send()
    for j in range(n_shot):
        o = lax.rem(shot + n_shot - j, n_shot)
        share(j, rep).wait_send()
        swap(RET.at[1 - rep, o], PSW.at[o], j).wait_send()


def run_window(model, accum, own, aper, start, adj, wave, src, rec, obs):
    n_shot = lax.axis_size("shot")
    n_sub = lax.axis_size("sub")
    vm = pl.BlockSpec(memory_space=pltpu.VMEM)
    sm = pl.BlockSpec(memory_space=pltpu.SMEM)
    hbm = pl.BlockSpec(memory_space=pltpu.HBM)
    layer = (DEPTH, LANES)
    half = TILES // 2
    dma = pltpu.SemaphoreType.DMA
    halo = pltpu.VMEM((5, 4) + layer, F32)
    rim = dma((5,))

    def vmem(*shape):
        return pltpu.VMEM(shape, F32)

    chunk = (TILE_Y, HALF, QAC)
    return pl.pallas_call(
        physics,
        out_shape=[jax.ShapeDtypeStruct(model.shape, F32)] * 2,
        in_specs=[hbm, hbm, vm, vm, hbm, hbm, sm, sm, vm, vm],
        out_specs=[vm, vm],
        scratch_shapes=[
            vmem(9, LX + 2, *layer), vmem(9, LX, *layer), vmem(6, LX + 2, *layer),
            vmem(3, LX + 2, *layer), vmem(LX, *layer), vmem(3, LX, *layer),
            vmem(6, LX, *layer), vmem(LX, *layer), vmem(2, LX, *layer), vmem(LX, *layer),
            halo, halo, halo, halo, rim, rim, rim, rim,
            vmem(3, LX, *layer), vmem(3, LX, *layer),
            vmem(n_shot * TILES, max(LANES, n_shot * HALF)),
            vmem(2 * n_shot, TILE_Y, HALF, SLAB_XT * LANES),
            vmem(n_shot, *chunk), vmem(2, n_shot, *chunk), vmem(2, n_shot, *chunk),
            vmem(n_shot, *chunk), vmem(n_shot, *chunk), vmem(n_shot, *chunk),
            vmem(2, TILE_Y, half, QAC), vmem(TILE_Y, half, QAC), vmem(TILE_Y, half, QAC),
            vmem(n_sub, TILE_Y, half, QAC), vmem(2, TILE_Y, half, QAC),
            dma((n_shot,)), dma((n_shot,)), dma((n_shot,)), dma((n_shot,)),
            dma((n_shot,)), dma((n_shot,)), dma((n_sub, TILE_Y)), dma((n_sub, TILE_Y)),
            dma((n_shot,)), dma((n_shot,)),
            vmem(*model.shape), vmem(*accum.shape),
            pltpu.VMEM(start.shape, start.dtype), pltpu.VMEM(adj.shape, adj.dtype),
            dma((4,)), dma((TILE_Y,)), dma((TILE_Y,)), dma((TILE_Y,)), dma((TILE_Y,)),
        ],
        compiler_params=pltpu.CompilerParams(
            collective_id=0, has_side_effects=True, vmem_limit_bytes=63 * 1024 * 1024),
    )(model, accum, own, aper, start, adj, wave, src, rec, obs)


def on_device(
    model, accum, owner_map, aperture, start_state, adjoint_end, wavelet, source_cell,
    receiver_cell, observed,
):
    start = start_state[0, 0, 0].transpose(0, 1, 3, 2)
    adj = adjoint_end[0, 0, 0].transpose(0, 1, 3, 2)
    new_model, new_accum = run_window(
        model.transpose(1, 0, 2), accum.transpose(1, 0, 2), owner_map.reshape(1, -1),
        aperture, start, adj, wavelet.reshape(NSTEPS), source_cell.reshape(1),
        receiver_cell.reshape(1, -1), observed[0, 0, 0],
    )
    return (new_model.transpose(1, 0, 2), new_accum.transpose(1, 0, 2))


def solution(mesh):
    in_specs = (
        P(("groups", "shot"), None, None),
        P(("groups", "shot"), None, None),
        P("groups"),
        P("groups", "sub", None),
        P(("groups", "shot"), "rep", None, None, "sub", None, None),
        P(("groups", "shot"), "rep", None, None, "sub", None, None),
        P(("groups", "shot"), "rep", None, None),
        P(("groups", "shot"), "rep", None),
        P(("groups", "shot"), "rep", None, None),
        P(("groups", "shot"), "rep", None, None, None),
    )
    out_specs = (P(("groups", "shot"), None, None), P(("groups", "shot"), None, None))
    return jax.shard_map(
        on_device, mesh=mesh, in_specs=in_specs, out_specs=out_specs, check_vma=False
    )
```

```python
import jax
import jax.numpy as jnp
from jax import lax
from jax.experimental import pallas as pl
from jax.experimental.pallas import tpu as pltpu
from jax.sharding import PartitionSpec as P

DEPTH = 32
TILE_X = 4
TILE_Y = 5
SLAB_XT = 2
SLAB_YT = 16
NSTEPS = 2
SLAB_TILES = 32
LX = SLAB_XT * TILE_X
WY = SLAB_YT * TILE_Y
LANES = 128

time_step = 0.18
learn_rate = 0.5
MESH = pl.DeviceIdType.MESH
F32 = jnp.float32
BF16 = jnp.bfloat16
TILES = 32
HALF = 8
QAC = 3 * TILE_X * DEPTH

TO_PRIOR = (2, 2, 1, 4, 1)
TO_NEXT = (4, 1, 2, 2, 2)


def next_y(f):
    return pltpu.roll(f, LANES - 1, 1)


def prior_y(f):
    return pltpu.roll(f, 1, 1)


def split3(v):
    hi = v.astype(BF16)
    rest = v - hi.astype(F32)
    mid = rest.astype(BF16)
    return hi, mid, (rest - mid.astype(F32)).astype(BF16)


def dot(x, y):
    return lax.dot_general(x, y, (((1,), (0,)), ((), ())), preferred_element_type=F32)


def dot_nt(x, y):
    return lax.dot_general(x, y, (((1,), (1,)), ((), ())), preferred_element_type=F32)


def onehot(mask):
    return jnp.where(mask, 1.0, 0.0).astype(BF16)


def iotas(rows, cols):
    return (lax.broadcasted_iota(jnp.int32, (rows, cols), 0),
            lax.broadcasted_iota(jnp.int32, (rows, cols), 1))


def physics(
    model_hbm, accum_hbm, own_ref, aper_ref,
    start_hbm, adj_hbm, wave_ref, src_ref, rec_ref, obs_ref, new_model_ref, new_accum_ref,
    F, C, W, A, B, DV, ST, CNT, OB, R0,
    send_l, send_r, recv_l, recv_r, ss_l, ss_r, rs_l, rs_r,
    par_ref, grad_ref, GT, Y, OUT, RECV, RET, PSW, RETS, ARR, TP, TW, TH, SB, TF,
    g_send, g_recv, p_send, p_recv, b_send, b_recv, x_send, x_recv, w_send, w_recv,
    model_ref, accum_ref, start_ref, adj_ref, l_sem, v_send, v_recv, y_send, y_recv,
):
    fetch = [
        pltpu.make_async_copy(src, dst, l_sem.at[i])
        for i, (src, dst) in enumerate([
            (model_hbm, model_ref), (start_hbm, start_ref), (adj_hbm, adj_ref),
            (accum_hbm, accum_ref)])
    ]
    for copy in fetch:
        copy.start()
    n_sub = lax.axis_size("sub")
    n_shot = lax.axis_size("shot")
    me = lax.axis_index("sub")
    shot = lax.axis_index("shot")
    rep = lax.axis_index("rep")
    partner = {"rep": 1 - rep}
    has_l = me > 0
    has_r = me < n_sub - 1
    left = {"sub": jnp.maximum(me - 1, 0)}
    right = {"sub": jnp.minimum(me + 1, n_sub - 1)}
    barrier = pltpu.get_barrier_semaphore()
    others = [{"shot": lax.rem(shot + j, n_shot)} for j in range(1, n_shot)]
    others += [{"sub": lax.rem(me + j, n_sub)} for j in range(1, n_sub)]
    others += [partner]
    for other in others:
        pl.semaphore_signal(barrier, inc=1, device_id=other, device_id_type=MESH)

    n_slots = n_shot * TILES
    n_pos = n_shot * SLAB_TILES
    l8, l16 = max(LANES, n_shot * HALF), max(LANES, n_shot * 2 * HALF)
    r_, c_ = iotas(n_slots, own_ref.shape[1])
    perm = onehot(own_ref[...] == r_)
    r_, c_ = iotas(own_ref.shape[1], n_pos)
    ids = jnp.concatenate([aper_ref[s] for s in range(n_shot)], axis=1)
    named = onehot(ids == r_)
    at = dot(perm, named).astype(BF16)
    r_, c_ = iotas(n_slots, n_slots)
    lower = onehot((r_ // TILES == c_ // TILES) & (c_ < r_))
    r_, c_ = iotas(n_pos, l8)
    occ = dot(at, onehot(r_ // SLAB_TILES == c_ // HALF))
    rank = dot(lower, occ.astype(BF16))
    r_, c_ = iotas(n_slots, l8)
    place = (rep * HALF + c_ % HALF).astype(F32)
    GT[...] = jnp.where(rank == place, occ, 0.0)
    gt = GT[pl.ds(pl.multiple_of(shot * TILES, TILES), TILES)]
    g = gt.T[: n_shot * HALF].astype(BF16)
    gt = gt[:, : n_shot * HALF].astype(BF16)
    fetch[0].wait()
    columns = []
    for b in range(TILE_Y):
        for k in range(3):
            columns.append(jnp.concatenate(
                [model_ref[k, :, pl.ds((a * TILE_Y + b) * DEPTH, DEPTH)] for a in range(TILE_X)],
                axis=1))
    flat = jnp.concatenate(columns, axis=1)
    outgoing = dot(jnp.concatenate([g, g, g], axis=1), jnp.concatenate(split3(flat), axis=0))
    for b in range(TILE_Y):
        OUT[:, b] = outgoing[:, b * QAC:(b + 1) * QAC].reshape(n_shot, HALF, QAC)

    pl.semaphore_wait(barrier, len(others))

    def gather(j):
        return pltpu.make_async_remote_copy(
            src_ref=OUT.at[lax.rem(shot + j, n_shot)], dst_ref=RECV.at[rep, shot],
            send_sem=g_send.at[j], recv_sem=g_recv.at[j],
            device_id={"shot": lax.rem(shot + j, n_shot)}, device_id_type=MESH)

    def gather_in(j):
        came = RECV.at[rep, lax.rem(shot + n_shot - j, n_shot)]
        return pltpu.make_async_remote_copy(
            src_ref=came, dst_ref=came, send_sem=g_send.at[j], recv_sem=g_recv.at[j],
            device_id={"shot": lax.rem(shot + j, n_shot)}, device_id_type=MESH)

    def share(j, half):
        came = RECV.at[half, lax.rem(shot + n_shot - j, n_shot)]
        return pltpu.make_async_remote_copy(
            src_ref=came, dst_ref=came, send_sem=p_send.at[j], recv_sem=p_recv.at[j],
            device_id=partner, device_id_type=MESH)

    for j in range(n_shot - 1, 0, -1):
        gather(j).start()
    RECV[rep, shot] = OUT[shot]
    share(0, rep).start()

    def copies(e):
        nl, nr = TO_PRIOR[e], TO_NEXT[e]
        to_l = pltpu.make_async_remote_copy(
            src_ref=send_l.at[e, pl.ds(0, nl)], dst_ref=recv_r.at[e, pl.ds(0, nl)],
            send_sem=ss_l.at[e], recv_sem=rs_r.at[e], device_id=left, device_id_type=MESH)
        to_r = pltpu.make_async_remote_copy(
            src_ref=send_r.at[e, pl.ds(0, nr)], dst_ref=recv_l.at[e, pl.ds(0, nr)],
            send_sem=ss_r.at[e], recv_sem=rs_l.at[e], device_id=right, device_id_type=MESH)
        return to_l, to_r

    def send(e, firsts, lasts):
        to_l, to_r = copies(e)

        @pl.when(has_l)
        def _():
            for k, (ref, i) in enumerate(firsts):
                send_l[e, k] = ref[i, 1]
            to_l.start()

        @pl.when(has_r)
        def _():
            for k, (ref, i) in enumerate(lasts):
                send_r[e, k] = ref[i, LX]
            to_r.start()

    def receive(e, firsts, lasts):
        to_l, to_r = copies(e)

        @pl.when(has_r)
        def _():
            to_r.wait_send()
            to_l.wait_recv()
            for k, (ref, i) in enumerate(firsts):
                ref[i, LX + 1] = recv_r[e, k]

        @pl.when(has_l)
        def _():
            to_l.wait_send()
            to_r.wait_recv()
            for k, (ref, i) in enumerate(lasts):
                ref[i, 0] = recv_l[e, k]

    zrow = lax.broadcasted_iota(jnp.int32, (DEPTH, LANES), 0)
    lane = lax.broadcasted_iota(jnp.int32, (DEPTH, LANES), 1)
    inside = lane < WY

    def next_z(f):
        return jnp.where(zrow == DEPTH - 1, 0.0, pltpu.roll(f, DEPTH - 1, 0))

    def prior_z(f):
        return jnp.where(zrow == 0, 0.0, pltpu.roll(f, 1, 0))

    def py(f):
        return next_y(f) - f

    def my(f):
        return f - prior_y(f)

    def pz(f):
        return next_z(f) - f

    def mz(f):
        return f - prior_z(f)

    def px(ref, i, x):
        return ref[i, x + 1] - ref[i, x]

    def mx(ref, i, x):
        return ref[i, x] - ref[i, x - 1]

    zero = jnp.zeros((DEPTH, LANES), F32)

    def strain_cot(x, c):
        lame = par_ref[0, x - 1]
        shear = par_ref[1, x - 1]
        trace = time_step * lame * (c[0] + c[1] + c[2])
        ds = time_step * shear
        W[0, x] = trace + 2.0 * ds * c[0]
        W[1, x] = trace + 2.0 * ds * c[1]
        W[2, x] = trace + 2.0 * ds * c[2]
        W[3, x] = ds * c[3]
        W[4, x] = ds * c[4]
        W[5, x] = ds * c[5]

    def edges_first(body, after):
        body(1)
        body(LX)
        after()
        lax.fori_loop(2, LX, lambda x, _: (body(x), 0)[1], 0)

    for i in range(9):
        F[i, 0] = zero
        F[i, LX + 1] = zero
    for i in range(6):
        W[i, 0] = zero
        W[i, LX + 1] = zero
    for i in range(3):
        A[i, 0] = zero
        A[i, LX + 1] = zero

    def load(x):
        for i in range(9):
            F[i, x] = zero
            F[i, x, :, pl.ds(0, WY)] = start_ref[i, x - 1].astype(F32)
            C[i, x - 1] = zero
            C[i, x - 1, :, pl.ds(0, WY)] = adj_ref[i, x - 1].astype(F32)

    def with_model(x):
        B[x - 1] = jnp.where(inside, 1.0 / jnp.where(inside, par_ref[2, x - 1], 1.0), 0.0)
        strain_cot(x, [C[3 + i, x - 1] for i in range(6)])

    e0 = ([(F, 3), (W, 0)], [(F, 6), (F, 7), (W, 3), (W, 4)])
    e1 = ([(F, 1), (F, 2)], [(F, 0)])
    e2 = ([(F, 3)], [(F, 6), (F, 7)])
    e3 = ([(F, 1), (F, 2), (A, 1), (A, 2)], [(F, 0), (A, 0)])
    e4 = ([(W, 0)], [(W, 3), (W, 4)])

    fetch[1].wait()
    fetch[2].wait()
    lax.fori_loop(1, LX + 1, lambda x, _: (load(x), 0)[1], 0)
    cell = rec_ref[...]
    q = cell >> 5
    rx = (q * 52429) >> 22
    ry = q - rx * WY
    rrow = (rx - me * LX) * DEPTH + (cell & (DEPTH - 1))
    nrec = rec_ref.shape[1]
    rows = lax.broadcasted_iota(jnp.int32, (LX * DEPTH, nrec), 0)
    cols = lax.broadcasted_iota(jnp.int32, (LANES, nrec), 0)
    at_row = onehot(rows == rrow)
    at_col = cols == ry

    def spread(values):
        out = None
        for piece in split3(values):
            term = dot_nt(at_row, jnp.where(at_col, piece.astype(F32), 0.0).astype(BF16))
            out = term if out is None else out + term
        return out

    count = dot_nt(at_row, onehot(at_col))
    CNT[...] = count.reshape(LX, DEPTH, LANES)
    OB[0] = spread(obs_ref[0:1]).reshape(LX, DEPTH, LANES)
    OB[1] = spread(obs_ref[1:2]).reshape(LX, DEPTH, LANES)

    r_, c_ = iotas(n_pos, l16)
    occ = dot(at, onehot(r_ // SLAB_TILES == shot))
    rank = dot(lower, occ.astype(BF16))
    r_, c_ = iotas(n_slots, l16)
    half_of = c_ // (n_shot * HALF)
    owner_of = c_ // HALF - half_of * n_shot
    place = (half_of * HALF + c_ % HALF).astype(F32)
    chunk = jnp.where((rank == place) & (owner_of == r_ // TILES), occ, 0.0)
    r_, c_ = iotas(n_pos, SLAB_XT * LANES)
    pos = r_ % SLAB_TILES
    in_y = c_ % LANES
    cover = (r_ // SLAB_TILES == shot) & (pos // SLAB_YT == c_ // LANES)
    cover = cover & (pos % SLAB_YT == in_y // TILE_Y)
    cells_of = dot(at, onehot(cover)).astype(BF16)
    where_ = dot(chunk.T.astype(BF16), cells_of)[: 2 * n_shot * HALF]
    r_, c_ = iotas(2 * n_shot * HALF, SLAB_XT * LANES)
    for b in range(TILE_Y):
        part = jnp.where(c_ % LANES % TILE_Y == b, where_, 0.0)
        Y[:, b] = part.reshape(2 * n_shot, HALF, SLAB_XT * LANES)
    k_rows = 2 * n_shot * TILE_Y * HALF
    ymat = Y[...].reshape(k_rows, SLAB_XT * LANES).astype(BF16)

    for j in range(1, n_shot):
        gather_in(j).wait_recv()
        share(j, rep).start()
    for j in range(n_shot):
        share(j, 1 - rep).wait_recv()
    came = RECV[...].reshape(k_rows, QAC).T
    slab = None
    for piece in split3(came):
        term = dot(piece, ymat)
        slab = term if slab is None else slab + term
    for k in range(3):
        for a in range(TILE_X):
            for i in range(SLAB_XT):
                par_ref[k, i * TILE_X + a] = slab[
                    (k * TILE_X + a) * DEPTH:(k * TILE_X + a + 1) * DEPTH,
                    i * LANES:(i + 1) * LANES]
    edges_first(with_model, lambda: send(0, *e0))

    scell = src_ref[0]
    sq = scell >> 5
    sx = (sq * 52429) >> 22
    sy = sq - sx * WY
    sz = scell & (DEPTH - 1)
    at_src = jnp.where((zrow == sz) & (lane == sy), 1.0, 0.0)

    def divergence(x):
        return [
            px(F, 3, x) + my(F[6, x]) + mz(F[7, x]),
            mx(F, 6, x) + py(F[4, x]) + mz(F[8, x]),
            mx(F, 7, x) + my(F[8, x]) + pz(F[5, x]),
        ]

    def strains(x):
        vx, vy, vz = F[0, x], F[1, x], F[2, x]
        return [
            mx(F, 0, x), my(vy), mz(vz),
            py(vx) + px(F, 1, x), pz(vx) + px(F, 2, x), pz(vy) + py(vz),
        ]

    def velocity_cot(x):
        exx, eyy, ezz = W[0, x], W[1, x], W[2, x]
        gxy, gxz, gyz = W[3, x], W[4, x], W[5, x]
        return [
            px(W, 0, x) + my(gxy) + mz(gxz),
            py(eyy) + mx(W, 3, x) + mz(gyz),
            pz(ezz) + mx(W, 4, x) + my(gyz),
        ]

    def first_velocity(x):
        b = time_step * B[x - 1]
        d = divergence(x)
        for i in range(3):
            DV[i, x - 1] = d[i]
            F[i, x] = F[i, x] + b * d[i]
        R0[x - 1] = CNT[x - 1] * F[2, x] - OB[0, x - 1]

    receive(0, *e0)
    edges_first(first_velocity, lambda: send(1, *e1))

    def first_stress(x):
        lame = time_step * par_ref[0, x - 1]
        shear = time_step * par_ref[1, x - 1]
        s = strains(x)
        for i in range(6):
            ST[i, x - 1] = s[i]
        amp = jnp.where(x - 1 + me * LX == sx, time_step * wave_ref[0], 0.0)
        base = lame * (s[0] + s[1] + s[2]) + amp * at_src
        for i in range(3):
            F[3 + i, x] = F[3 + i, x] + (base + 2.0 * shear * s[i])
            F[6 + i, x] = F[6 + i, x] + shear * s[3 + i]

    receive(1, *e1)
    edges_first(first_stress, lambda: send(2, *e2))

    def second_velocity(x):
        inv = B[x - 1]
        b = time_step * inv
        d = divergence(x)
        w = velocity_cot(x)
        for i in range(3):
            F[i, x] = F[i, x] + b * d[i]
        res = CNT[x - 1] * F[2, x] - OB[1, x - 1]
        total = zero
        for i in range(3):
            c = C[i, x - 1] - w[i]
            if i == 2:
                c = c + res
            C[i, x - 1] = c
            a = b * c
            A[i, x] = a
            total = total + a * d[i]
        grad_ref[2, x - 1] = -inv * total

    receive(2, *e2)
    edges_first(second_velocity, lambda: send(3, *e3))

    def model_part(c, s):
        part_lame = (s[0] + s[1] + s[2]) * (c[0] + c[1] + c[2])
        part_shear = 2.0 * (s[0] * c[0] + s[1] * c[1] + s[2] * c[2]) + (
            s[3] * c[3] + s[4] * c[4] + s[5] * c[5])
        return part_lame, part_shear

    def stress_back(x):
        c = [C[3 + i, x - 1] for i in range(6)]
        lame1, shear1 = model_part(c, strains(x))
        ax, ay, az = A[0, x], A[1, x], A[2, x]
        c = [
            c[0] - mx(A, 0, x),
            c[1] - my(ay),
            c[2] - mz(az),
            c[3] - py(ax) - px(A, 1, x),
            c[4] - pz(ax) - px(A, 2, x),
            c[5] - pz(ay) - py(az),
        ]
        strain_cot(x, c)
        lame0, shear0 = model_part(c, [ST[i, x - 1] for i in range(6)])
        grad_ref[0, x - 1] = time_step * (lame1 + lame0)
        grad_ref[1, x - 1] = time_step * (shear1 + shear0)

    receive(3, *e3)
    edges_first(stress_back, lambda: send(4, *e4))

    def last_velocity(x):
        inv = B[x - 1]
        b = time_step * inv
        w = velocity_cot(x)
        total = zero
        for i in range(3):
            c = C[i, x - 1] - w[i]
            if i == 2:
                c = c + R0[x - 1]
            total = total + b * c * DV[i, x - 1]
        grad_ref[2, x - 1] = grad_ref[2, x - 1] - inv * total

    receive(4, *e4)
    lax.fori_loop(1, LX + 1, lambda x, _: (last_velocity(x), 0)[1], 0)


    rows_ = []
    for k in range(3):
        for a in range(TILE_X):
            rows_.append(jnp.concatenate(
                [grad_ref[k, i * TILE_X + a] for i in range(SLAB_XT)], axis=1))
    rows_ = jnp.concatenate(rows_, axis=0)
    back = None
    for piece in split3(rows_):
        term = dot_nt(ymat, piece)
        back = term if back is None else back + term
    RET[...] = back.reshape(2, n_shot, TILE_Y, HALF, QAC)

    def swap(src, dst, k):
        return pltpu.make_async_remote_copy(
            src_ref=src, dst_ref=dst, send_sem=w_send.at[k], recv_sem=w_recv.at[k],
            device_id=partner, device_id_type=MESH)

    for j in range(n_shot):
        o = lax.rem(shot + n_shot - j, n_shot)
        swap(RET.at[1 - rep, o], PSW.at[o], j).start()

    def give(j):
        return pltpu.make_async_remote_copy(
            src_ref=RETS.at[lax.rem(shot + n_shot - j, n_shot)], dst_ref=ARR.at[shot],
            send_sem=b_send.at[j], recv_sem=b_recv.at[j],
            device_id={"shot": lax.rem(shot + n_shot - j, n_shot)}, device_id_type=MESH)

    def give_in(j):
        o = lax.rem(shot + j, n_shot)
        return pltpu.make_async_remote_copy(
            src_ref=ARR.at[o], dst_ref=ARR.at[o], send_sem=b_send.at[j],
            recv_sem=b_recv.at[j], device_id={"shot": o}, device_id_type=MESH)

    for j in list(range(1, n_shot)) + [0]:
        o = lax.rem(shot + n_shot - j, n_shot)
        swap(RET.at[1 - rep, o], PSW.at[o], j).wait_recv()
        if j > 0:
            RETS[o] = RET[rep, o] + PSW[o]
            give(j).start()
        else:
            ARR[o] = RET[rep, o] + PSW[o]
    for j in range(1, n_shot):
        give_in(j).wait_recv()
    ggg = jnp.concatenate([gt, gt, gt], axis=1)
    half_rows = TILES // 2

    def to_core(b):
        return pltpu.make_async_remote_copy(
            src_ref=TP.at[1 - rep, b], dst_ref=TW.at[b], send_sem=v_send.at[b],
            recv_sem=v_recv.at[b], device_id=partner, device_id_type=MESH)

    def across(j, b):
        return pltpu.make_async_remote_copy(
            src_ref=SB.at[me, b], dst_ref=SB.at[me, b], send_sem=x_send.at[j, b],
            recv_sem=x_recv.at[j, b], device_id={"sub": lax.rem(me + j, n_sub)},
            device_id_type=MESH)

    def across_in(j, b):
        u = lax.rem(me + n_sub - j, n_sub)
        return pltpu.make_async_remote_copy(
            src_ref=SB.at[u, b], dst_ref=SB.at[u, b], send_sem=x_send.at[j, b],
            recv_sem=x_recv.at[j, b], device_id={"sub": lax.rem(me + j, n_sub)},
            device_id_type=MESH)

    def last(b, half):
        return pltpu.make_async_remote_copy(
            src_ref=TH.at[b], dst_ref=TF.at[half, b], send_sem=y_send.at[b],
            recv_sem=y_recv.at[b], device_id=partner, device_id_type=MESH)

    for b in range(TILE_Y):
        arrived = ARR[:, b].reshape(n_shot * HALF, QAC)
        part = dot(ggg, jnp.concatenate(split3(arrived), axis=0))
        TP[0, b] = part[:half_rows]
        TP[1, b] = part[half_rows:]
        to_core(b).start()
    for b in range(TILE_Y):
        to_core(b).wait_recv()
        SB[me, b] = TP[rep, b] + TW[b]
        for j in range(1, n_sub):
            across(j, b).start()
    for b in range(TILE_Y):
        for j in range(1, n_sub):
            across_in(j, b).wait_recv()
        total = SB[0, b]
        for u in range(1, n_sub):
            total = total + SB[u, b]
        TF[rep, b] = total
        TH[b] = total
        last(b, rep).start()
    fetch[3].wait()
    for b in range(TILE_Y):
        last(b, 1 - rep).wait_recv()

    for k in range(3):
        for h in range(2):
            grad = jnp.concatenate(
                [TF[h, b, :, pl.ds((k * TILE_X + a) * DEPTH, DEPTH)]
                 for a in range(TILE_X) for b in range(TILE_Y)], axis=1)
            rows = pl.ds(h * half_rows, half_rows)
            new_accum = accum_ref[k, rows] + grad * grad
            new_accum_ref[k, rows] = new_accum
            new_model_ref[k, rows] = model_ref[k, rows] - learn_rate * grad / jnp.sqrt(new_accum)

    for b in range(TILE_Y):
        last(b, rep).wait_send()
        to_core(b).wait_send()
        for j in range(1, n_sub):
            across(j, b).wait_send()
    for j in range(1, n_shot):
        gather(j).wait_send()
        give(j).wait_send()
    for j in range(n_shot):
        o = lax.rem(shot + n_shot - j, n_shot)
        share(j, rep).wait_send()
        swap(RET.at[1 - rep, o], PSW.at[o], j).wait_send()


def run_window(model, accum, own, aper, start, adj, wave, src, rec, obs):
    n_shot = lax.axis_size("shot")
    n_sub = lax.axis_size("sub")
    vm = pl.BlockSpec(memory_space=pltpu.VMEM)
    sm = pl.BlockSpec(memory_space=pltpu.SMEM)
    hbm = pl.BlockSpec(memory_space=pltpu.HBM)
    layer = (DEPTH, LANES)
    half = TILES // 2
    dma = pltpu.SemaphoreType.DMA
    halo = pltpu.VMEM((5, 4) + layer, F32)
    rim = dma((5,))

    def vmem(*shape):
        return pltpu.VMEM(shape, F32)

    chunk = (TILE_Y, HALF, QAC)
    return pl.pallas_call(
        physics,
        out_shape=[jax.ShapeDtypeStruct(model.shape, F32)] * 2,
        in_specs=[hbm, hbm, vm, vm, hbm, hbm, sm, sm, vm, vm],
        out_specs=[vm, vm],
        scratch_shapes=[
            vmem(9, LX + 2, *layer), vmem(9, LX, *layer), vmem(6, LX + 2, *layer),
            vmem(3, LX + 2, *layer), vmem(LX, *layer), vmem(3, LX, *layer),
            vmem(6, LX, *layer), vmem(LX, *layer), vmem(2, LX, *layer), vmem(LX, *layer),
            halo, halo, halo, halo, rim, rim, rim, rim,
            vmem(3, LX, *layer), vmem(3, LX, *layer),
            vmem(n_shot * TILES, max(LANES, n_shot * HALF)),
            vmem(2 * n_shot, TILE_Y, HALF, SLAB_XT * LANES),
            vmem(n_shot, *chunk), vmem(2, n_shot, *chunk), vmem(2, n_shot, *chunk),
            vmem(n_shot, *chunk), vmem(n_shot, *chunk), vmem(n_shot, *chunk),
            vmem(2, TILE_Y, half, QAC), vmem(TILE_Y, half, QAC), vmem(TILE_Y, half, QAC),
            vmem(n_sub, TILE_Y, half, QAC), vmem(2, TILE_Y, half, QAC),
            dma((n_shot,)), dma((n_shot,)), dma((n_shot,)), dma((n_shot,)),
            dma((n_shot,)), dma((n_shot,)), dma((n_sub, TILE_Y)), dma((n_sub, TILE_Y)),
            dma((n_shot,)), dma((n_shot,)),
            vmem(*model.shape), vmem(*accum.shape),
            pltpu.VMEM(start.shape, start.dtype), pltpu.VMEM(adj.shape, adj.dtype),
            dma((4,)), dma((TILE_Y,)), dma((TILE_Y,)), dma((TILE_Y,)), dma((TILE_Y,)),
        ],
        compiler_params=pltpu.CompilerParams(
            collective_id=0, has_side_effects=True, vmem_limit_bytes=63 * 1024 * 1024),
    )(model, accum, own, aper, start, adj, wave, src, rec, obs)


def on_device(
    model, accum, owner_map, aperture, start_state, adjoint_end, wavelet, source_cell,
    receiver_cell, observed,
):
    start = start_state[0, 0, 0].transpose(0, 1, 3, 2)
    adj = adjoint_end[0, 0, 0].transpose(0, 1, 3, 2)
    new_model, new_accum = run_window(
        model.transpose(1, 0, 2), accum.transpose(1, 0, 2), owner_map.reshape(1, -1),
        aperture, start, adj, wavelet.reshape(NSTEPS), source_cell.reshape(1),
        receiver_cell.reshape(1, -1), observed[0, 0, 0],
    )
    return (new_model.transpose(1, 0, 2), new_accum.transpose(1, 0, 2))


def solution(mesh):
    in_specs = (
        P(("groups", "shot"), None, None),
        P(("groups", "shot"), None, None),
        P("groups"),
        P("groups", "sub", None),
        P(("groups", "shot"), "rep", None, None, "sub", None, None),
        P(("groups", "shot"), "rep", None, None, "sub", None, None),
        P(("groups", "shot"), "rep", None, None),
        P(("groups", "shot"), "rep", None),
        P(("groups", "shot"), "rep", None, None),
        P(("groups", "shot"), "rep", None, None, None),
    )
    out_specs = (P(("groups", "shot"), None, None), P(("groups", "shot"), None, None))
    return jax.shard_map(
        on_device, mesh=mesh, in_specs=in_specs, out_specs=out_specs, check_vma=False
    )
```
